256 devices in a mesh: pair: 32 (over z, y), cd: 8 (over x, core).
Axes of the slice: x: 4, y: 4, z: 8, core: 2. Of those that a mesh axis runs over, the one named last changes fastest.
Arguments:
- amplitudes: bfloat16 [8192, 4096], P('pair', 'cd'), may hold values from -6 to 6
- integrals: bfloat16 [2, 8192, 4096], P(None, 'pair', 'cd'), may hold values from -0.1875 to 0.1875
- row_irreps: int32 [32, 2], P('pair'), may hold values from 0 to 3
- col_irreps: int32 [16, 2], P('cd'), may hold values from 0 to 3
Outputs:
- sigma: bfloat16 [8192, 8192], P('cd', 'pair')
The draws below stay inside these ranges and needn't reach their ends.
All inputs are finite; a program needn't handle non-finite values.
Results may differ from the reference program's by a relative error of at most 0.014.
Values may be sent and summed in bfloat16 or wider, within the bound.
A program may use at most 192 MiB of HBM per device.

```python
import jax
import jax.numpy as jnp
from jax import lax

TP = 256
NCOL = 8192
P_SIZE = 8192
Q = 4096
N_CD = 8


def place_ends(values, stream_key, least, largest):
    longest = values.shape.index(max(values.shape))
    spots = []
    for shift in (0, 1):
        where = [jax.random.randint(jax.random.fold_in(stream_key, axis), (), 0, length) for axis, length in enumerate(values.shape)]
        where[longest] = (where[longest] + shift) % values.shape[longest]
        spots.append(tuple(where))
    return values.at[spots[0]].set(least).at[spots[1]].set(largest)


def block_levels(own_key, dims, shards, smallest, high):
    level = 1.0
    for position, parts in shards:
        heights = jax.random.uniform(jax.random.fold_in(jax.random.fold_in(own_key, 6), position), (parts,), jnp.float32, smallest / len(shards), high / len(shards))
        level = level * jnp.repeat(jnp.exp(heights), dims[position] // parts).reshape((-1,) + (1,) * (len(dims) - 1 - position))
    return level


def scatter_about(key, shape, deviation, limit, split=(), held_as=jnp.bfloat16):
    values = jax.random.normal(key, shape, jnp.float32) * deviation
    if len(split) > 0:
        values = block_levels(key, shape, split, -0.22, 0.18) * values
    return jnp.clip(values, min=-limit, max=limit).astype(held_as)


def setup_inputs(seed: int = 0) -> dict:
    seeds = jax.random.split(jax.random.key(seed), 5)
    return {
        "amplitudes": scatter_about(seeds[0], (NCOL, Q), 1.0, 6.0, ((0, 32), (1, 8))),
        "integrals": scatter_about(seeds[1], (2, P_SIZE, Q), (Q // 4) ** -0.5, 0.1875, ((1, 32), (2, 8))),
        "row_irreps": place_ends(jax.random.randint(seeds[2], (P_SIZE // TP, 2), 0, 4), jax.random.fold_in(seeds[2], 1), 0, 3).astype(jnp.int32),
        "col_irreps": place_ends(jax.random.randint(seeds[3], (Q // TP, 2), 0, 4), jax.random.fold_in(seeds[3], 1), 0, 3).astype(jnp.int32),
    }


def pair_symmetry(labels):
    return jnp.bitwise_xor(labels[:, 0], labels[:, 1])


def reference(amplitudes, integrals, row_irreps, col_irreps):
    half_rows = NCOL // 2
    block_cols = Q // N_CD
    row_sym = pair_symmetry(row_irreps)
    col_sym = pair_symmetry(col_irreps)
    direct = amplitudes[:half_rows].astype(jnp.float32)
    mirrored = amplitudes[half_rows:].astype(jnp.float32)
    packed = jnp.concatenate([direct + mirrored, direct - mirrored], 0).astype(jnp.bfloat16)
    packed = lax.optimization_barrier(packed).astype(jnp.float32)
    packed = packed.reshape(2, half_rows, N_CD, block_cols)

    def row_tile(index):
        weights = lax.dynamic_slice_in_dim(integrals, index * TP, TP, 1).astype(jnp.float32)
        keep = (col_sym == row_sym[index]).astype(jnp.float32)
        weights = weights * jnp.repeat(keep, TP)[None, None, :]
        weights = weights.reshape(2, TP, N_CD, block_cols)
        terms = jnp.einsum("hcks,hpks->hkcp", packed, weights, precision=lax.Precision.HIGHEST)
        combined = jnp.stack([terms[0] + terms[1], terms[0] - terms[1]], 0)
        rounded = lax.optimization_barrier(combined.astype(jnp.bfloat16)).astype(jnp.float32)
        totals = jnp.sum(rounded, axis=1)
        return totals.reshape(NCOL, TP).astype(jnp.bfloat16)

    blocks = lax.map(row_tile, jnp.arange(P_SIZE // TP, dtype=jnp.int32))
    return jnp.transpose(blocks, (1, 0, 2)).reshape(NCOL, P_SIZE)
```

```python
import functools

import jax
import jax.numpy as jnp
from jax import lax
from jax.experimental import pallas as pl
from jax.experimental.pallas import tpu as pltpu
from jax.sharding import PartitionSpec as P

MESH = pl.DeviceIdType.MESH
NX, NY, NZ = 4, 4, 8

CHUNKS = (64, 64, 64, 64)

STEPS = None


def coordinates():
    pair, cd = lax.axis_index("pair"), lax.axis_index("cd")
    return lax.div(cd, 2), lax.rem(pair, NY), lax.div(pair, NY), lax.rem(cd, 2)


def kernel(
    steps, amp, integ, row_ir, col_ir, out,
    ag, asib, pk, wb, cp, sx1, rx1, sx2, rx2, res,
    loc, zs, zr, ds, dr, ys, yr, ws, wr, x1s, x1r, x2s, x2r, os, orr,
):
    x, y, z, c = coordinates()
    sib = 1 - c
    chunks = CHUNKS
    starts = [sum(chunks[:k]) for k in range(len(chunks))]
    tiles = {}
    offset = 0
    for r, n in enumerate(chunks):
        for g in range(4):
            tiles[r, g] = (len(tiles), offset)
            offset += n

    def dev(dx=0, dy=0, dz=0, flip=False):
        return (
            lax.rem(z + dz + NZ, NZ) * NY + lax.rem(y + dy + NY, NY),
            lax.rem(x + dx + NX, NX) * 2 + (sib if flip else c),
        )

    load_a = pltpu.make_async_copy(amp, ag.at[z], loc.at[0])
    load_w = pltpu.make_async_copy(integ, wb.at[0, :, :, pl.ds(0, 512)], loc.at[1])
    load_a.start()
    load_w.start()
    barrier = pltpu.get_barrier_semaphore()
    partners = [
        dev(dx=1), dev(dx=-1), dev(dy=1), dev(dy=-1), dev(dy=2), dev(dz=1), dev(dz=-1), dev(flip=True),
    ]
    for partner in partners:
        pl.semaphore_signal(barrier, inc=1, device_id=partner, device_id_type=MESH)
    started = []

    def remote(src, dst, send, recv, to):
        return pltpu.make_async_remote_copy(
            src_ref=src, dst_ref=dst, send_sem=send, recv_sem=recv, device_id=to, device_id_type=MESH
        )

    def go(copy):
        copy.start()
        started.append(copy)

    def z_rows(r, s, d):
        if d < 4:
            return pl.ds(starts[r], chunks[r])
        half = chunks[r] // 2
        return pl.ds(starts[r] + (0 if s == 0 else half), half)

    def z_copy(r, s, d, behind):
        sign = 1 if s == 0 else -1
        block = ag.at[lax.rem(z - sign * behind + NZ, NZ), z_rows(r, s, d)]
        return remote(block, block, zs.at[r, s, d - 1], zr.at[r, s, d - 1], dev(dz=sign))

    def z_send(r, d):
        for s in (0, 1):
            go(z_copy(r, s, d, d - 1))

    def z_wait(r, d):
        for s in (0, 1):
            z_copy(r, s, d, d).wait_recv()

    def y_half(s, n):
        return s if n != 1 else 1 - s

    def y_copy(s, n):
        sign = 1 if s == 0 else -1
        half = pl.ds(128 * y_half(s, n), 128)
        src = wb.at[0 if n < 2 else 1, :, half, pl.ds(0, 512)]
        dst = wb.at[n + 1, :, half, pl.ds(0, 512)]
        return remote(src, dst, ys.at[s, n], yr.at[s, n], dev(dy=sign))

    def w_give(g):
        return remote(
            wb.at[g, :, :, pl.ds(0, 512)], wb.at[g, :, :, pl.ds(512, 512)], ws.at[g], wr.at[g], dev(flip=True)
        )

    def a_give(r):
        rows = pl.ds(starts[r], chunks[r])
        src = ag.reshape(4, 2, 256, 512).at[:, sib, rows]
        return remote(src, asib.at[:, rows], ds.at[r], dr.at[r], dev(flip=True))

    def x1_copy(r, g, s):
        t, off = tiles[r, g]
        half = chunks[r] // 2
        rows = pl.ds(off + s * half, half)
        return remote(
            sx1.at[rows], rx1.at[rows], x1s.at[t, s], x1r.at[t, s], dev(dx=1 if s == 0 else -1)
        )

    def x2_copy(r, g, s):
        t, off = tiles[r, g]
        rows = pl.ds(off, chunks[r])
        return remote(
            sx2.at[s, rows], rx2.at[s, rows], x2s.at[t, s], x2r.at[t, s], dev(dx=1 if s == 0 else -1)
        )

    def owner(g, h):
        return {1: (-1, 1), 2: (1, -1), 3: (2, 2)}[g][h]

    def o_copy(r, g, h, origin, to):
        t, off = tiles[r, g]
        cols = pl.ds(128 * h, 128)
        dst = out.at[pl.ds(pl.multiple_of(origin * 256 + starts[r], 32), chunks[r]), cols]
        return remote(res.at[pl.ds(off, chunks[r]), cols], dst, os.at[t, h], orr.at[t, h], to)

    def multiply(r, g):
        t, off = tiles[r, g]
        n = chunks[r]
        rows = pl.ds(2 * starts[r], 2 * n)
        dims = (((1,), (1,)), ((), ()))
        plus = lax.dot_general(pk[0, rows], wb[g, 0], dims, preferred_element_type=jnp.float32)
        minus = lax.dot_general(pk[1, rows], wb[g, 1], dims, preferred_element_type=jnp.float32)
        upper, lower = plus + minus, plus - minus
        own = pl.ds(off, n)
        cp[0, own] = upper[:n]
        cp[1, own] = upper[n:]
        cp[2, own] = lower[:n]
        cp[3, own] = lower[n:]
        sx1[own] = cp[lax.rem(x + 2, NX), own].astype(jnp.bfloat16)
        for s in (0, 1):
            go(x1_copy(r, g, s))

    def add_on(r, g):
        t, off = tiles[r, g]
        n = chunks[r]
        half = n // 2
        for s in (0, 1):
            x1_copy(r, g, s).wait_recv()
            target = lax.rem(x + (1 if s == 0 else 3), NX)
            for k in (0, 1):
                part = pl.ds(off + k * half, half)
                value = cp[target, part]
                if k == s:
                    value = value + rx1[part].astype(jnp.float32)
                sx2[s, part] = value.astype(jnp.bfloat16)
            go(x2_copy(r, g, s))

    def finish(r, g):
        t, off = tiles[r, g]
        n = chunks[r]
        own = pl.ds(off, n)
        for s in (0, 1):
            x2_copy(r, g, s).wait_recv()
        total = cp[x, own] + rx2[0, own].astype(jnp.float32) + rx2[1, own].astype(jnp.float32)
        total = total.astype(jnp.bfloat16)
        if g == 0:
            out[pl.ds(pl.multiple_of(y * 256 + starts[r], 32), n)] = total
        else:
            res[own] = total
            for h in (0, 1):
                go(o_copy(r, g, h, y, dev(dy=owner(g, h))))

    def pack(r):
        a_give(r).wait_recv()
        n = chunks[r]
        rows = pl.ds(starts[r], n)
        for i in (0, 1):
            to = pl.ds(2 * starts[r] + i * n, n)
            for k, (direct, mirror) in enumerate((
                (ag[c + 2 * i, rows], ag[c + 2 * i + 4, rows]),
                (asib[i, rows], asib[i + 2, rows]),
            )):
                direct, mirror = direct.astype(jnp.float32), mirror.astype(jnp.float32)
                cols = pl.ds(512 * k, 512)
                pk[0, to, cols] = (direct + mirror).astype(jnp.bfloat16)
                pk[1, to, cols] = (direct - mirror).astype(jnp.bfloat16)

    load_a.wait()
    load_w.wait()
    row_sym = row_ir[0, 0] ^ row_ir[0, 1]
    for k in (0, 1):
        keep = (row_sym == (col_ir[k, 0] ^ col_ir[k, 1])).astype(jnp.int32).astype(jnp.float32)
        cols = pl.ds(256 * k, 256)
        for s in (0, 1):
            wb[0, s, :, cols] = (wb[0, s, :, cols].astype(jnp.float32) * keep).astype(jnp.bfloat16)
    pl.semaphore_wait(barrier, len(partners))

    for step in steps:
        name, args = step[0], step[1:]
        if name == "zo":
            z_send(args[0], 1)
        elif name == "zf":
            z_wait(*args)
            z_send(args[0], args[1] + 1)
        elif name == "zc":
            z_wait(args[0], 4)
            go(a_give(args[0]))
        elif name == "pk":
            pack(*args)
        elif name == "wo":
            for s in (0, 1):
                go(y_copy(s, args[0]))
        elif name == "wg":
            go(w_give(0))
        elif name == "wf":
            for s in (0, 1):
                y_copy(s, args[0]).wait_recv()
            if args[0] == 0:
                for s in (0, 1):
                    go(y_copy(s, 2))
            go(w_give(args[0] + 1))
        elif name == "ws":
            w_give(args[0]).wait_recv()
        elif name == "mm":
            multiply(*args)
        elif name == "ra":
            add_on(*args)
        elif name == "fi":
            finish(*args)
    for r in range(len(chunks)):
        for g in (1, 2, 3):
            for h in (0, 1):
                back = owner(g, h)
                origin = lax.rem(y - back + NY, NY)
                o_copy(r, g, h, origin, dev(dy=back)).wait_recv()
    for copy in started:
        copy.wait_send()


STEPS = [
    ("zo", 0), ("wo", 0), ("zo", 1), ("wg",), ("wo", 1), ("zf", 0, 1), ("zo", 2), ("zf", 0, 2), ("zf", 1, 1),
    ("wf", 0), ("zf", 0, 3), ("zo", 3), ("ws", 0), ("zc", 0), ("zf", 1, 2), ("ws", 1), ("pk", 0), ("mm", 0, 0), ("zf", 2, 1),
    ("mm", 0, 1), ("zf", 1, 3), ("ra", 0, 0), ("wf", 1), ("ra", 0, 1), ("fi", 0, 0), ("zf", 2, 2), ("fi", 0, 1),
    ("zc", 1), ("ws", 2), ("mm", 0, 2), ("zf", 3, 1), ("pk", 1), ("mm", 1, 0), ("ra", 0, 2), ("zf", 2, 3), ("mm", 1, 1),
    ("ra", 1, 0), ("fi", 0, 2), ("mm", 1, 2), ("zf", 3, 2), ("ra", 1, 1), ("zc", 2), ("fi", 1, 0), ("ra", 1, 2), ("wf", 2), ("fi", 1, 1),
    ("pk", 2), ("mm", 2, 0), ("fi", 1, 2), ("zf", 3, 3), ("mm", 2, 1), ("ws", 3), ("ra", 2, 0), ("mm", 2, 2), ("ra", 2, 1), ("fi", 2, 0),
    ("mm", 0, 3), ("ra", 2, 2), ("zc", 3), ("fi", 2, 1), ("mm", 1, 3), ("ra", 0, 3), ("fi", 2, 2), ("mm", 2, 3), ("ra", 1, 3), ("fi", 0, 3),
    ("pk", 3), ("mm", 3, 0), ("ra", 2, 3), ("fi", 1, 3), ("mm", 3, 1), ("ra", 3, 0), ("fi", 2, 3), ("mm", 3, 2), ("ra", 3, 1), ("fi", 3, 0),
    ("mm", 3, 3), ("ra", 3, 2), ("fi", 3, 1), ("ra", 3, 3), ("fi", 3, 2), ("fi", 3, 3),
]


def on_device(amplitudes, integrals, row_irreps, col_irreps):
    count, bf16, dma = len(CHUNKS), jnp.bfloat16, pltpu.SemaphoreType.DMA
    any_space, smem, vmem = (pl.BlockSpec(memory_space=s) for s in (pl.ANY, pltpu.SMEM, pltpu.VMEM))
    return pl.pallas_call(
        functools.partial(kernel, STEPS),
        out_shape=jax.ShapeDtypeStruct((1024, 256), bf16),
        in_specs=[any_space, any_space, smem, smem],
        out_specs=vmem,
        scratch_shapes=[
            pltpu.VMEM((8, 256, 512), bf16),
            pltpu.VMEM((4, 256, 512), bf16),
            pltpu.VMEM((2, 512, 1024), bf16),
            pltpu.VMEM((4, 2, 256, 1024), bf16),
            pltpu.VMEM((4, 1024, 256), jnp.float32),
            pltpu.VMEM((1024, 256), bf16),
            pltpu.VMEM((1024, 256), bf16),
            pltpu.VMEM((2, 1024, 256), bf16),
            pltpu.VMEM((2, 1024, 256), bf16),
            pltpu.VMEM((1024, 256), bf16),
            dma((2,)),
            dma((count, 2, 4)), dma((count, 2, 4)),
            dma((count,)), dma((count,)),
            dma((2, 3)), dma((2, 3)),
            dma((4,)), dma((4,)),
            dma((4 * count, 2)), dma((4 * count, 2)),
            dma((4 * count, 2)), dma((4 * count, 2)),
            dma((4 * count, 2)), dma((4 * count, 2)),
        ],
        compiler_params=pltpu.CompilerParams(
            collective_id=0, has_side_effects=True, vmem_limit_bytes=48 * 2**20
        ),
        cost_estimate=pl.CostEstimate(flops=2 * 2**30, bytes_accessed=2 * 2**20, transcendentals=0),
        name="ladder",
    )(amplitudes, integrals, row_irreps, col_irreps)


def solution(mesh):
    in_specs = (P("pair", "cd"), P(None, "pair", "cd"), P("pair", None), P("cd", None))
    out_specs = P("cd", "pair")
    return jax.shard_map(
        on_device, mesh=mesh, in_specs=in_specs, out_specs=out_specs, check_vma=False
    )
```

```python
import functools

import jax
import jax.numpy as jnp
from jax import lax
from jax.experimental import pallas as pl
from jax.experimental.pallas import tpu as pltpu
from jax.sharding import PartitionSpec as P

MESH = pl.DeviceIdType.MESH
NX, NY, NZ = 4, 4, 8

CHUNKS = (64, 64, 64, 64)

STEPS = None


def coordinates():
    pair, cd = lax.axis_index("pair"), lax.axis_index("cd")
    return lax.div(cd, 2), lax.rem(pair, NY), lax.div(pair, NY), lax.rem(cd, 2)


def kernel(
    steps, amp, integ, row_hbm, col_hbm, out, row_ir, col_ir,
    ag, asib, pk, wb, cp, sx1, rx1, sx2, rx2, res,
    loc, zs, zr, zq, ds, dr, ys, yr, ws, wr, x1s, x1r, x2s, x2r, os, orr,
):
    x, y, z, c = coordinates()
    sib = 1 - c
    chunks = CHUNKS
    starts = [sum(chunks[:k]) for k in range(len(chunks))]
    tiles = {}
    offset = 0
    for r, n in enumerate(chunks):
        for g in range(4):
            tiles[r, g] = (len(tiles), offset)
            offset += n

    def dev(dx=0, dy=0, dz=0, flip=False):
        return (
            lax.rem(z + dz + NZ, NZ) * NY + lax.rem(y + dy + NY, NY),
            lax.rem(x + dx + NX, NX) * 2 + (sib if flip else c),
        )

    load_a = pltpu.make_async_copy(amp, ag.at[z], loc.at[0])
    load_w = pltpu.make_async_copy(integ, wb.at[0, :, :, pl.ds(0, 512)], loc.at[1])
    loads = [
        load_w, load_a,
        pltpu.make_async_copy(row_hbm, row_ir, loc.at[2]),
        pltpu.make_async_copy(col_hbm, col_ir, loc.at[3]),
    ]
    for load in loads:
        load.start()
    barrier = pltpu.get_barrier_semaphore()
    partners = [
        dev(dx=1), dev(dx=-1), dev(dy=1), dev(dy=-1), dev(dy=2), dev(dz=1), dev(dz=-1), dev(flip=True),
    ]
    for partner in partners:
        pl.semaphore_signal(barrier, inc=1, device_id=partner, device_id_type=MESH)
    started = []

    def remote(src, dst, send, recv, to):
        return pltpu.make_async_remote_copy(
            src_ref=src, dst_ref=dst, send_sem=send, recv_sem=recv, device_id=to, device_id_type=MESH
        )

    def go(copy):
        copy.start()
        started.append(copy)

    mine = lax.rem(z, 2) == c

    def z_rows(r, s, d):
        if d < 4:
            return pl.ds(starts[r], chunks[r])
        half = chunks[r] // 2
        return pl.ds(starts[r] + (0 if s == 0 else half), half)

    def z_copy(r, s, d, behind):
        sign = 1 if s == 0 else -1
        block = ag.at[lax.rem(z - sign * behind + NZ, NZ), z_rows(r, s, d)]
        return remote(block, block, zs.at[r, s, d - 1], zr.at[r, s, d - 1], dev(dz=sign))

    def cross_copy(r, s, behind):
        sign = 1 if s == 0 else -1
        origin = lax.rem(z - sign * behind + NZ, NZ)
        rows = z_rows(r, s, 4)
        return remote(
            ag.at[origin, rows], asib.at[lax.div(origin, 2), rows], zs.at[r, s, 3], zq.at[r, s], dev(dz=sign, flip=True)
        )

    def z_send(r, d):
        for s in (0, 1):
            copy = z_copy(r, s, d, d - 1)
            if d < 4:
                go(copy)
            else:
                pl.when(jnp.logical_not(mine))(copy.start)
                pl.when(mine)(cross_copy(r, s, 3).start)
                started.append(copy)

    def z_wait(r, d):
        for s in (0, 1):
            z_copy(r, s, d, d).wait_recv()

    def share(r, e, far):
        origin = lax.rem(z + far + NZ, NZ)
        rows = pl.ds(starts[r], chunks[r])
        return remote(
            ag.at[origin, rows], asib.at[lax.div(origin, 2), rows], ds.at[r, e], dr.at[r, e], dev(flip=True)
        )

    def give(r, d):
        sends = {0: ((2, 0),), 1: ((0, 1), (1, -1)), 2: ((0, 2), (1, -2)), 3: ((2, 3), (3, -3))}[d]
        def act():
            for e, far in sends:
                share(r, e, far).start()
        pl.when(mine if d % 2 else jnp.logical_not(mine))(act)

    def y_half(s, n):
        return s if n != 1 else 1 - s

    def y_copy(s, n):
        sign = 1 if s == 0 else -1
        half = pl.ds(128 * y_half(s, n), 128)
        src = wb.at[0 if n < 2 else 1, :, half, pl.ds(0, 512)]
        dst = wb.at[n + 1, :, half, pl.ds(0, 512)]
        return remote(src, dst, ys.at[s, n], yr.at[s, n], dev(dy=sign))

    def w_give(g):
        return remote(
            wb.at[g, :, :, pl.ds(0, 512)], wb.at[g, :, :, pl.ds(512, 512)], ws.at[g], wr.at[g], dev(flip=True)
        )

    def x1_copy(r, g, s):
        t, off = tiles[r, g]
        rows = pl.ds(off, chunks[r])
        return remote(
            sx1.at[s, rows], rx1.at[s, rows], x1s.at[t, s], x1r.at[t, s], dev(dx=1 if s == 0 else -1)
        )

    def x2_copy(r, g, s):
        t, off = tiles[r, g]
        rows = pl.ds(off // 2, chunks[r] // 2)
        return remote(
            sx2.at[s, rows], rx2.at[s, rows], x2s.at[t, s], x2r.at[t, s], dev(dx=1 if s == 0 else -1)
        )

    def owner(g, h):
        return {1: (-1, 1), 2: (1, -1), 3: (2, 2)}[g][h]

    def o_copy(r, g, h, origin, to):
        t, off = tiles[r, g]
        cols = pl.ds(128 * h, 128)
        dst = out.at[pl.ds(pl.multiple_of(origin * 256 + starts[r], 32), chunks[r]), cols]
        return remote(res.at[pl.ds(off, chunks[r]), cols], dst, os.at[t, h], orr.at[t, h], to)

    def multiply(r, g):
        t, off = tiles[r, g]
        n = chunks[r]
        rows = pl.ds(2 * starts[r], 2 * n)
        dims = (((1,), (1,)), ((), ()))
        plus = lax.dot_general(pk[0, rows], wb[g, 0], dims, preferred_element_type=jnp.float32)
        minus = lax.dot_general(pk[1, rows], wb[g, 1], dims, preferred_element_type=jnp.float32)
        upper, lower = plus + minus, plus - minus
        own = pl.ds(off, n)
        cp[0, own] = upper[:n]
        cp[1, own] = upper[n:]
        cp[2, own] = lower[:n]
        cp[3, own] = lower[n:]
        half = n // 2
        for s in (0, 1):
            target = lax.rem(x + (1 if s == 0 else 3), NX)
            sx1[s, pl.ds(off, half)] = cp[lax.rem(x + 2, NX), pl.ds(off + s * half, half)].astype(jnp.bfloat16)
            sx1[s, pl.ds(off + half, half)] = cp[target, pl.ds(off + (1 - s) * half, half)].astype(jnp.bfloat16)
            go(x1_copy(r, g, s))

    def add_on(r, g):
        t, off = tiles[r, g]
        half = chunks[r] // 2
        for s in (0, 1):
            x1_copy(r, g, s).wait_recv()
            target = lax.rem(x + (1 if s == 0 else 3), NX)
            value = cp[target, pl.ds(off + s * half, half)] + rx1[s, pl.ds(off, half)].astype(jnp.float32)
            sx2[s, pl.ds(off // 2, half)] = value.astype(jnp.bfloat16)
            go(x2_copy(r, g, s))

    def finish(r, g):
        t, off = tiles[r, g]
        n = chunks[r]
        half = n // 2
        for s in (0, 1):
            x2_copy(r, g, s).wait_recv()
        for s in (0, 1):
            total = (
                cp[x, pl.ds(off + s * half, half)]
                + rx2[s, pl.ds(off // 2, half)].astype(jnp.float32)
                + rx1[1 - s, pl.ds(off + half, half)].astype(jnp.float32)
            ).astype(jnp.bfloat16)
            if g == 0:
                out[pl.ds(pl.multiple_of(y * 256 + starts[r] + s * half, 16), half)] = total
            else:
                res[pl.ds(off + s * half, half)] = total
        if g > 0:
            for h in (0, 1):
                go(o_copy(r, g, h, y, dev(dy=owner(g, h))))

    def pack(r):
        for e in (0, 1, 2):
            share(r, e, 0).wait_recv()
        pl.when(jnp.logical_not(mine))(share(r, 3, 0).wait_recv)
        def last_hop():
            for s in (0, 1):
                z_copy(r, s, 4, 4).wait_recv()
                cross_copy(r, s, 4).wait_recv()
        pl.when(mine)(last_hop)
        n = chunks[r]
        rows = pl.ds(starts[r], n)
        for i in (0, 1):
            to = pl.ds(2 * starts[r] + i * n, n)
            for k, (direct, mirror) in enumerate((
                (ag[c + 2 * i, rows], ag[c + 2 * i + 4, rows]),
                (asib[i, rows], asib[i + 2, rows]),
            )):
                direct, mirror = direct.astype(jnp.float32), mirror.astype(jnp.float32)
                cols = pl.ds(512 * k, 512)
                pk[0, to, cols] = (direct + mirror).astype(jnp.bfloat16)
                pk[1, to, cols] = (direct - mirror).astype(jnp.bfloat16)

    for load in loads:
        load.wait()
    row_sym = row_ir[0, 0] ^ row_ir[0, 1]
    for k in (0, 1):
        keep = (row_sym == (col_ir[k, 0] ^ col_ir[k, 1])).astype(jnp.int32).astype(jnp.float32)
        cols = pl.ds(256 * k, 256)
        for s in (0, 1):
            wb[0, s, :, cols] = (wb[0, s, :, cols].astype(jnp.float32) * keep).astype(jnp.bfloat16)
    pl.semaphore_wait(barrier, len(partners))

    for step in steps:
        name, args = step[0], step[1:]
        if name == "zo":
            z_send(args[0], 1)
            give(args[0], 0)
        elif name == "zf":
            z_wait(*args)
            z_send(args[0], args[1] + 1)
            give(*args)
        elif name == "pk":
            pack(*args)
        elif name == "wo":
            for s in (0, 1):
                go(y_copy(s, args[0]))
        elif name == "wg":
            go(w_give(0))
        elif name == "wf":
            for s in (0, 1):
                y_copy(s, args[0]).wait_recv()
            if args[0] == 0:
                for s in (0, 1):
                    go(y_copy(s, 2))
            go(w_give(args[0] + 1))
        elif name == "ws":
            w_give(args[0]).wait_recv()
        elif name == "mm":
            multiply(*args)
        elif name == "ra":
            add_on(*args)
        elif name == "fi":
            finish(*args)
    for r in range(len(chunks)):
        for g in (1, 2, 3):
            for h in (0, 1):
                back = owner(g, h)
                origin = lax.rem(y - back + NY, NY)
                o_copy(r, g, h, origin, dev(dy=back)).wait_recv()
    for r in range(len(chunks)):
        for e in (0, 1, 2):
            share(r, e, 0).wait_send()
        pl.when(mine)(share(r, 3, 0).wait_send)
    for copy in started:
        copy.wait_send()


STEPS = [
    ("wo", 0), ("zo", 0), ("wg",), ("zo", 1), ("wo", 1), ("zo", 2), ("ws", 0), ("zf", 0, 1), ("zf", 1, 1), ("zo", 3),
    ("wf", 0), ("zf", 0, 2), ("zf", 1, 2), ("ws", 1), ("zf", 0, 3), ("zf", 2, 1), ("wf", 1), ("zf", 1, 3),
    ("zf", 3, 1), ("pk", 0), ("ws", 2), ("mm", 0, 1), ("mm", 0, 2), ("zf", 2, 2), ("mm", 0, 0), ("pk", 1),
    ("mm", 1, 1), ("mm", 1, 2), ("zf", 3, 2), ("mm", 1, 0), ("wf", 2), ("ra", 0, 1), ("zf", 2, 3), ("ra", 0, 2),
    ("ra", 0, 0), ("ra", 1, 1), ("ws", 3), ("mm", 0, 3), ("zf", 3, 3), ("ra", 1, 2), ("mm", 1, 3), ("ra", 1, 0),
    ("pk", 2), ("fi", 0, 1), ("mm", 2, 1), ("fi", 0, 2), ("fi", 0, 0), ("mm", 2, 2), ("fi", 1, 1), ("ra", 0, 3),
    ("pk", 3), ("mm", 2, 3), ("fi", 1, 2), ("ra", 1, 3), ("mm", 3, 1), ("fi", 1, 0), ("mm", 3, 2), ("ra", 2, 1),
    ("mm", 3, 3), ("ra", 2, 2), ("fi", 0, 3), ("ra", 2, 3), ("mm", 2, 0), ("fi", 1, 3), ("ra", 3, 1), ("mm", 3, 0),
    ("ra", 3, 2), ("fi", 2, 1), ("ra", 3, 3), ("fi", 2, 2), ("fi", 2, 3), ("ra", 2, 0), ("fi", 3, 1), ("ra", 3, 0),
    ("fi", 3, 2), ("fi", 3, 3), ("fi", 2, 0), ("fi", 3, 0),
]


def on_device(amplitudes, integrals, row_irreps, col_irreps):
    count, bf16, dma = len(CHUNKS), jnp.bfloat16, pltpu.SemaphoreType.DMA
    hbm, vmem = (pl.BlockSpec(memory_space=s) for s in (pltpu.HBM, pltpu.VMEM))
    return pl.pallas_call(
        functools.partial(kernel, STEPS),
        out_shape=jax.ShapeDtypeStruct((1024, 256), bf16),
        in_specs=[hbm] * 4,
        out_specs=vmem,
        scratch_shapes=[
            pltpu.SMEM((1, 2), jnp.int32),
            pltpu.SMEM((2, 2), jnp.int32),
            pltpu.VMEM((8, 256, 512), bf16),
            pltpu.VMEM((4, 256, 512), bf16),
            pltpu.VMEM((2, 512, 1024), bf16),
            pltpu.VMEM((4, 2, 256, 1024), bf16),
            pltpu.VMEM((4, 1024, 256), jnp.float32),
            pltpu.VMEM((2, 1024, 256), bf16),
            pltpu.VMEM((2, 1024, 256), bf16),
            pltpu.VMEM((2, 512, 256), bf16),
            pltpu.VMEM((2, 512, 256), bf16),
            pltpu.VMEM((1024, 256), bf16),
            dma((4,)),
            dma((count, 2, 4)), dma((count, 2, 4)), dma((count, 2)),
            dma((count, 4)), dma((count, 4)),
            dma((2, 3)), dma((2, 3)),
            dma((4,)), dma((4,)),
            dma((4 * count, 2)), dma((4 * count, 2)),
            dma((4 * count, 2)), dma((4 * count, 2)),
            dma((4 * count, 2)), dma((4 * count, 2)),
        ],
        compiler_params=pltpu.CompilerParams(
            collective_id=0, has_side_effects=True, vmem_limit_bytes=56 * 2**20
        ),
        cost_estimate=pl.CostEstimate(flops=2 * 2**30, bytes_accessed=2 * 2**20, transcendentals=0),
        name="ladder",
    )(amplitudes, integrals, row_irreps, col_irreps)


def solution(mesh):
    in_specs = (P("pair", "cd"), P(None, "pair", "cd"), P("pair", None), P("cd", None))
    out_specs = P("cd", "pair")
    return jax.shard_map(
        on_device, mesh=mesh, in_specs=in_specs, out_specs=out_specs, check_vma=False
    )
```

```python
import functools

import jax
import jax.numpy as jnp
from jax import lax
from jax.experimental import pallas as pl
from jax.experimental.pallas import tpu as pltpu
from jax.sharding import PartitionSpec as P

MESH = pl.DeviceIdType.MESH
NX, NY, NZ = 4, 4, 8

CHUNKS = (64, 64, 64, 64)

STEPS = None


def coordinates():
    pair, cd = lax.axis_index("pair"), lax.axis_index("cd")
    return lax.div(cd, 2), lax.rem(pair, NY), lax.div(pair, NY), lax.rem(cd, 2)


def kernel(
    steps, amp, integ, row_hbm, col_hbm, out, row_ir, col_ir,
    ag, asib, pk, wb, cp, sx1, rx1, sx2, rx2, res,
    loc, sent, zr, pr, yr, wr, x1r, x2r, orr,
):
    x, y, z, c = coordinates()
    sib = 1 - c
    chunks = CHUNKS
    starts = [sum(chunks[:k]) for k in range(len(chunks))]
    tiles = {}
    offset = 0
    for r, n in enumerate(chunks):
        for g in range(4):
            tiles[r, g] = (len(tiles), offset)
            offset += n

    def dev(dx=0, dy=0, dz=0, flip=False):
        return (
            lax.rem(z + dz + NZ, NZ) * NY + lax.rem(y + dy + NY, NY),
            lax.rem(x + dx + NX, NX) * 2 + (sib if flip else c),
        )

    load_a = pltpu.make_async_copy(amp, ag.at[z], loc.at[0])
    load_w = pltpu.make_async_copy(integ, wb.at[0, :, :, pl.ds(0, 512)], loc.at[1])
    loads = [
        load_w, load_a,
        pltpu.make_async_copy(row_hbm, row_ir, loc.at[2]),
        pltpu.make_async_copy(col_hbm, col_ir, loc.at[3]),
    ]
    for load in loads:
        load.start()
    barrier = pltpu.get_barrier_semaphore()
    partners = [
        dev(dx=1), dev(dx=-1), dev(dy=1), dev(dy=-1), dev(dy=2), dev(dz=1), dev(dz=-1), dev(flip=True),
    ]
    for partner in partners:
        pl.semaphore_signal(barrier, inc=1, device_id=partner, device_id_type=MESH)
    def remote(src, dst, send, recv, to):
        return pltpu.make_async_remote_copy(
            src_ref=src, dst_ref=dst, send_sem=send, recv_sem=recv, device_id=to, device_id_type=MESH
        )

    def arrived(ref, recv):
        remote(ref, ref, sent.at[0], recv, dev(flip=True)).wait_recv()

    def left(ref, send):
        remote(ref, ref, sent.at[send], orr, dev(flip=True)).wait_send()

    mine = lax.rem(z, 2) == c

    def z_rows(r, s, d):
        if d < 4:
            return pl.ds(starts[r], chunks[r])
        half = chunks[r] // 2
        return pl.ds(starts[r] + (0 if s == 0 else half), half)

    def z_copy(r, s, d, behind):
        sign = 1 if s == 0 else -1
        block = ag.at[lax.rem(z - sign * behind + NZ, NZ), z_rows(r, s, d)]
        return remote(block, block, sent.at[0], zr.at[r, d - 1] if d < 4 else pr.at[r], dev(dz=sign))

    def cross_copy(r, s, behind):
        sign = 1 if s == 0 else -1
        origin = lax.rem(z - sign * behind + NZ, NZ)
        rows = z_rows(r, s, 4)
        return remote(
            ag.at[origin, rows], asib.at[lax.div(origin, 2), rows], sent.at[0], pr.at[r], dev(dz=sign, flip=True)
        )

    def z_send(r, d):
        for s in (0, 1):
            copy = z_copy(r, s, d, d - 1)
            if d < 4:
                copy.start()
            else:
                pl.when(jnp.logical_not(mine))(copy.start)
                pl.when(mine)(cross_copy(r, s, 3).start)

    def z_wait(r, d):
        arrived(ag.at[pl.ds(0, 2), z_rows(r, 0, d)], zr.at[r, d - 1])

    def share(r, far):
        origin = lax.rem(z + far + NZ, NZ)
        rows = pl.ds(starts[r], chunks[r])
        return remote(
            ag.at[origin, rows], asib.at[lax.div(origin, 2), rows], sent.at[1], pr.at[r], dev(flip=True)
        )

    def give(r, d):
        sends = {0: (0,), 1: (1, -1), 2: (2, -2), 3: (3, -3)}[d]
        def act():
            for far in sends:
                share(r, far).start()
        pl.when(mine if d % 2 else jnp.logical_not(mine))(act)

    def y_half(s, n):
        return s if n != 1 else 1 - s

    def y_copy(s, n):
        sign = 1 if s == 0 else -1
        half = pl.ds(128 * y_half(s, n), 128)
        src = wb.at[0 if n < 2 else 1, :, half, pl.ds(0, 512)]
        dst = wb.at[n + 1, :, half, pl.ds(0, 512)]
        return remote(src, dst, sent.at[2], yr.at[n], dev(dy=sign))

    def w_give(g):
        return remote(
            wb.at[g, :, :, pl.ds(0, 512)], wb.at[g, :, :, pl.ds(512, 512)], sent.at[3], wr.at[g], dev(flip=True)
        )

    def x1_copy(r, g, s):
        t, off = tiles[r, g]
        rows = pl.ds(off, chunks[r])
        return remote(
            sx1.at[s, rows], rx1.at[s, rows], sent.at[4], x1r.at[t], dev(dx=1 if s == 0 else -1)
        )

    def x2_copy(r, g, s):
        t, off = tiles[r, g]
        rows = pl.ds(off // 2, chunks[r] // 2)
        return remote(
            sx2.at[s, rows], rx2.at[s, rows], sent.at[5], x2r.at[t], dev(dx=1 if s == 0 else -1)
        )

    def owner(g, h):
        return {1: (-1, 1), 2: (1, -1), 3: (2, 2)}[g][h]

    def o_copy(r, g, h, origin, to):
        t, off = tiles[r, g]
        cols = pl.ds(128 * h, 128)
        dst = out.at[pl.ds(pl.multiple_of(origin * 256 + starts[r], 32), chunks[r]), cols]
        return remote(res.at[pl.ds(off, chunks[r]), cols], dst, sent.at[6], orr, to)

    def multiply(r, g):
        t, off = tiles[r, g]
        n = chunks[r]
        rows = pl.ds(2 * starts[r], 2 * n)
        dims = (((1,), (1,)), ((), ()))
        plus = lax.dot_general(pk[0, rows], wb[g, 0], dims, preferred_element_type=jnp.float32)
        minus = lax.dot_general(pk[1, rows], wb[g, 1], dims, preferred_element_type=jnp.float32)
        upper, lower = plus + minus, plus - minus
        own = pl.ds(off, n)
        cp[0, own] = upper[:n]
        cp[1, own] = upper[n:]
        cp[2, own] = lower[:n]
        cp[3, own] = lower[n:]
        half = n // 2
        for s in (0, 1):
            target = lax.rem(x + (1 if s == 0 else 3), NX)
            sx1[s, pl.ds(off, half)] = cp[lax.rem(x + 2, NX), pl.ds(off + s * half, half)].astype(jnp.bfloat16)
            sx1[s, pl.ds(off + half, half)] = cp[target, pl.ds(off + (1 - s) * half, half)].astype(jnp.bfloat16)
            x1_copy(r, g, s).start()

    def add_on(r, g):
        t, off = tiles[r, g]
        half = chunks[r] // 2
        arrived(rx1.at[:, pl.ds(off, chunks[r])], x1r.at[t])
        for s in (0, 1):
            target = lax.rem(x + (1 if s == 0 else 3), NX)
            value = cp[target, pl.ds(off + s * half, half)] + rx1[s, pl.ds(off, half)].astype(jnp.float32)
            sx2[s, pl.ds(off // 2, half)] = value.astype(jnp.bfloat16)
            x2_copy(r, g, s).start()

    def finish(r, g):
        t, off = tiles[r, g]
        n = chunks[r]
        half = n // 2
        arrived(rx2.at[:, pl.ds(off // 2, half)], x2r.at[t])
        for s in (0, 1):
            total = (
                cp[x, pl.ds(off + s * half, half)]
                + rx2[s, pl.ds(off // 2, half)].astype(jnp.float32)
                + rx1[1 - s, pl.ds(off + half, half)].astype(jnp.float32)
            ).astype(jnp.bfloat16)
            if g == 0:
                out[pl.ds(pl.multiple_of(y * 256 + starts[r] + s * half, 16), half)] = total
            else:
                res[pl.ds(off + s * half, half)] = total
        if g > 0:
            for h in (0, 1):
                o_copy(r, g, h, y, dev(dy=owner(g, h))).start()

    def pack(r):
        rows = pl.ds(starts[r], chunks[r])
        pl.when(mine)(lambda: arrived(ag.at[pl.ds(0, 5), rows], pr.at[r]))
        pl.when(jnp.logical_not(mine))(lambda: arrived(ag.at[pl.ds(0, 4), rows], pr.at[r]))
        n = chunks[r]
        for i in (0, 1):
            to = pl.ds(2 * starts[r] + i * n, n)
            for k, (direct, mirror) in enumerate((
                (ag[c + 2 * i, rows], ag[c + 2 * i + 4, rows]),
                (asib[i, rows], asib[i + 2, rows]),
            )):
                direct, mirror = direct.astype(jnp.float32), mirror.astype(jnp.float32)
                cols = pl.ds(512 * k, 512)
                pk[0, to, cols] = (direct + mirror).astype(jnp.bfloat16)
                pk[1, to, cols] = (direct - mirror).astype(jnp.bfloat16)

    for load in loads:
        load.wait()
    row_sym = row_ir[0, 0] ^ row_ir[0, 1]
    for k in (0, 1):
        keep = (row_sym == (col_ir[k, 0] ^ col_ir[k, 1])).astype(jnp.int32).astype(jnp.float32)
        cols = pl.ds(256 * k, 256)
        for s in (0, 1):
            wb[0, s, :, cols] = (wb[0, s, :, cols].astype(jnp.float32) * keep).astype(jnp.bfloat16)
    pl.semaphore_wait(barrier, len(partners))

    for step in steps:
        name, args = step[0], step[1:]
        if name == "zo":
            z_send(args[0], 1)
            give(args[0], 0)
        elif name == "zf":
            z_wait(*args)
            z_send(args[0], args[1] + 1)
            give(*args)
        elif name == "pk":
            pack(*args)
        elif name == "wo":
            for s in (0, 1):
                y_copy(s, args[0]).start()
        elif name == "wg":
            w_give(0).start()
        elif name == "wf":
            arrived(wb.at[args[0] + 1, :, :, pl.ds(0, 512)], yr.at[args[0]])
            if args[0] == 0:
                for s in (0, 1):
                    y_copy(s, 2).start()
            w_give(args[0] + 1).start()
        elif name == "ws":
            w_give(args[0]).wait_recv()
        elif name == "mm":
            multiply(*args)
        elif name == "ra":
            add_on(*args)
        elif name == "fi":
            finish(*args)
    arrived(out.at[pl.ds(0, 768)], orr)
    left(ag.at[pl.ds(0, 7)], 0)
    pl.when(mine)(lambda: left(ag.at[pl.ds(0, 4)], 1))
    pl.when(jnp.logical_not(mine))(lambda: left(ag.at[pl.ds(0, 3)], 1))
    left(wb.at[pl.ds(0, 3), :, :, pl.ds(0, 512)], 2)
    left(wb.at[:, :, :, pl.ds(0, 512)], 3)
    left(sx1, 4)
    left(sx2, 5)
    left(res.at[pl.ds(0, 768)], 6)


STEPS = [
    ("wo", 0), ("zo", 0), ("wg",), ("zo", 1), ("wo", 1), ("zo", 2), ("ws", 0), ("zf", 0, 1), ("zf", 1, 1), ("zo", 3),
    ("wf", 0), ("zf", 0, 2), ("zf", 1, 2), ("ws", 1), ("zf", 0, 3), ("zf", 2, 1), ("wf", 1), ("zf", 1, 3),
    ("zf", 3, 1), ("pk", 0), ("ws", 2), ("mm", 0, 1), ("mm", 0, 2), ("zf", 2, 2), ("mm", 0, 0), ("pk", 1),
    ("mm", 1, 1), ("mm", 1, 2), ("zf", 3, 2), ("mm", 1, 0), ("wf", 2), ("ra", 0, 1), ("zf", 2, 3), ("ra", 0, 2),
    ("ra", 0, 0), ("ra", 1, 1), ("ws", 3), ("mm", 0, 3), ("zf", 3, 3), ("ra", 1, 2), ("mm", 1, 3), ("ra", 1, 0),
    ("pk", 2), ("fi", 0, 1), ("mm", 2, 1), ("fi", 0, 2), ("fi", 0, 0), ("mm", 2, 2), ("fi", 1, 1), ("ra", 0, 3),
    ("pk", 3), ("mm", 2, 3), ("fi", 1, 2), ("ra", 1, 3), ("mm", 3, 1), ("fi", 1, 0), ("mm", 3, 2), ("ra", 2, 1),
    ("mm", 3, 3), ("ra", 2, 2), ("fi", 0, 3), ("ra", 2, 3), ("mm", 2, 0), ("fi", 1, 3), ("ra", 3, 1), ("mm", 3, 0),
    ("ra", 3, 2), ("fi", 2, 1), ("ra", 3, 3), ("fi", 2, 2), ("fi", 2, 3), ("ra", 2, 0), ("fi", 3, 1), ("ra", 3, 0),
    ("fi", 3, 2), ("fi", 3, 3), ("fi", 2, 0), ("fi", 3, 0),
]


def on_device(amplitudes, integrals, row_irreps, col_irreps):
    count, bf16, dma = len(CHUNKS), jnp.bfloat16, pltpu.SemaphoreType.DMA
    hbm, vmem = (pl.BlockSpec(memory_space=s) for s in (pltpu.HBM, pltpu.VMEM))
    return pl.pallas_call(
        functools.partial(kernel, STEPS),
        out_shape=jax.ShapeDtypeStruct((1024, 256), bf16),
        in_specs=[hbm] * 4,
        out_specs=vmem,
        scratch_shapes=[
            pltpu.SMEM((1, 2), jnp.int32),
            pltpu.SMEM((2, 2), jnp.int32),
            pltpu.VMEM((8, 256, 512), bf16),
            pltpu.VMEM((4, 256, 512), bf16),
            pltpu.VMEM((2, 512, 1024), bf16),
            pltpu.VMEM((4, 2, 256, 1024), bf16),
            pltpu.VMEM((4, 1024, 256), jnp.float32),
            pltpu.VMEM((2, 1024, 256), bf16),
            pltpu.VMEM((2, 1024, 256), bf16),
            pltpu.VMEM((2, 512, 256), bf16),
            pltpu.VMEM((2, 512, 256), bf16),
            pltpu.VMEM((1024, 256), bf16),
            dma((4,)),
            dma((7,)), dma((count, 3)), dma((count,)), dma((3,)), dma((4,)), dma((4 * count,)), dma((4 * count,)), dma,
        ],
        compiler_params=pltpu.CompilerParams(
            collective_id=0, has_side_effects=True, vmem_limit_bytes=48 * 2**20
        ),
        cost_estimate=pl.CostEstimate(flops=2 * 2**30, bytes_accessed=2 * 2**20, transcendentals=0),
        name="ladder",
    )(*(pltpu.with_memory_space_constraint(a, pltpu.HBM) for a in (amplitudes, integrals, row_irreps, col_irreps)))


def solution(mesh):
    in_specs = (P("pair", "cd"), P(None, "pair", "cd"), P("pair", None), P("cd", None))
    out_specs = P("cd", "pair")
    return jax.shard_map(
        on_device, mesh=mesh, in_specs=in_specs, out_specs=out_specs, check_vma=False
    )
```

```python
import jax
import jax.numpy as jnp
from jax import lax
from jax.experimental import pallas as pl
from jax.experimental.pallas import tpu as pltpu
from jax.sharding import PartitionSpec as P

MESH = pl.DeviceIdType.MESH
NX, NY, NZ = 4, 4, 8

CHUNKS = (64, 64, 64, 64)


def coordinates():
    pair, cd = lax.axis_index("pair"), lax.axis_index("cd")
    return lax.div(cd, 2), lax.rem(pair, NY), lax.div(pair, NY), lax.rem(cd, 2)


def kernel(
    amp, integ, row_hbm, col_hbm, out, row_ir, col_ir,
    ag, asib, pk, wb, cp, sx1, rx1, sx2, rx2, res,
    loc, sent, zr, pa, pb, yr, wr, x1r, x2r, orr,
):
    x, y, z, c = coordinates()
    sib = 1 - c
    chunks = CHUNKS
    starts = [sum(chunks[:k]) for k in range(len(chunks))]
    def dev(dx=0, dy=0, dz=0, flip=False):
        return (
            lax.rem(z + dz + NZ, NZ) * NY + lax.rem(y + dy + NY, NY),
            lax.rem(x + dx + NX, NX) * 2 + (sib if flip else c),
        )

    load_a = pltpu.make_async_copy(amp, ag.at[z], loc.at[0])
    load_w = pltpu.make_async_copy(integ, wb.at[0, :, :, pl.ds(0, 512)], loc.at[1])
    loads = [
        load_w,
        pltpu.make_async_copy(row_hbm, row_ir, loc.at[2]),
        pltpu.make_async_copy(col_hbm, col_ir, loc.at[3]),
    ]
    load_a.start()
    for load in loads:
        load.start()
    barrier = pltpu.get_barrier_semaphore()
    partners = [
        dev(dx=1), dev(dx=-1), dev(dy=1), dev(dy=-1), dev(dy=2), dev(dz=1), dev(dz=-1), dev(flip=True),
    ]
    for partner in partners:
        pl.semaphore_signal(barrier, inc=1, device_id=partner, device_id_type=MESH)
    def remote(src, dst, send, recv, to):
        return pltpu.make_async_remote_copy(
            src_ref=src, dst_ref=dst, send_sem=send, recv_sem=recv, device_id=to, device_id_type=MESH
        )

    def arrived(ref, recv):
        remote(ref, ref, sent.at[0], recv, dev(flip=True)).wait_recv()

    def left(ref, send):
        remote(ref, ref, sent.at[send], orr, dev(flip=True)).wait_send()

    mine = lax.rem(z, 2) == c
    first = jnp.where(mine, 1 - lax.div(lax.rem(z, 4), 2), lax.div(lax.rem(z, 4), 2))

    def pair_of(e):
        return first if e == 0 else 1 - first

    def is_target(e):
        return lax.rem(x, 2) == pair_of(e)

    def z_rows(r, s, d):
        if d < 4:
            return pl.ds(starts[r], chunks[r])
        half = chunks[r] // 2
        return pl.ds(starts[r] + (0 if s == 0 else half), half)

    def z_copy(r, s, d, behind):
        sign = 1 if s == 0 else -1
        block = ag.at[lax.rem(z - sign * behind + NZ, NZ), z_rows(r, s, d)]
        return remote(block, block, sent.at[0], zr.at[r, d - 1] if d < 4 else pb.at[r], dev(dz=sign))

    def cross_copy(r, s, behind):
        sign = 1 if s == 0 else -1
        origin = lax.rem(z - sign * behind + NZ, NZ)
        rows = z_rows(r, s, 4)
        return remote(
            ag.at[origin, rows], asib.at[lax.div(origin, 2), rows], sent.at[0], pb.at[r], dev(dz=sign, flip=True)
        )

    def z_send(r, d):
        for s in (0, 1):
            copy = z_copy(r, s, d, d - 1)
            if d < 4:
                copy.start()
            else:
                pl.when(jnp.logical_not(mine))(copy.start)
                pl.when(mine)(cross_copy(r, s, 3).start)

    def z_wait(r, d):
        arrived(ag.at[pl.ds(0, 2), z_rows(r, 0, d)], zr.at[r, d - 1])

    def share(r, far):
        origin = lax.rem(z + far + NZ, NZ)
        rows = pl.ds(starts[r], chunks[r])
        return remote(
            ag.at[origin, rows], asib.at[lax.div(origin, 2), rows], sent.at[1], (pa if far else pb).at[r], dev(flip=True)
        )

    def give(r, d):
        sends = {0: (0,), 1: (1, -1), 2: (2, -2), 3: (3, -3)}[d]
        def act():
            for far in sends:
                share(r, far).start()
        pl.when(mine if d % 2 else jnp.logical_not(mine))(act)

    def y_half(s, n):
        return s if n != 1 else 1 - s

    def y_copy(s, n):
        sign = 1 if s == 0 else -1
        half = pl.ds(128 * y_half(s, n), 128)
        src = wb.at[0 if n < 2 else 1, :, half, pl.ds(0, 512)]
        dst = wb.at[n + 1, :, half, pl.ds(0, 512)]
        return remote(src, dst, sent.at[2], yr.at[n], dev(dy=sign))

    def w_give(g):
        return remote(
            wb.at[g, :, :, pl.ds(0, 512)], wb.at[g, :, :, pl.ds(512, 512)], sent.at[3], wr.at[g], dev(flip=True)
        )

    def x1_copy(t, s):
        rows = pl.ds(64 * t, 64)
        return remote(sx1.at[s, rows], rx1.at[s, rows], sent.at[4], x1r.at[t], dev(dx=1 if s == 0 else -1))

    def x2_copy(t, s):
        rows = pl.ds(64 * t, 64)
        return remote(sx2.at[s, rows], rx2.at[s, rows], sent.at[5], x2r.at[t], dev(dx=1 if s == 0 else -1))

    def owner(g, h):
        return {1: (-1, 1), 2: (1, -1), 3: (2, 2)}[g][h]

    def o_copy(b, g, h, to):
        cols = pl.ds(128 * h, 128)
        dst = out.at[pl.ds(pl.multiple_of(y * 256 + 128 * b, 128), 128), cols]
        return remote(res.at[pl.ds(128 * (4 * b + g), 128), cols], dst, sent.at[6], orr, to)

    def tile(b, e, g):
        return (2 * b + e) * 4 + g

    def block_of(dx):
        return lax.div(lax.rem(x + dx + NX, NX), 2)

    def pack(b, e):
        i = pair_of(e)
        for r in (2 * b, 2 * b + 1):
            rows = pl.ds(starts[r], chunks[r])
            if e == 0:
                pl.when(mine)(lambda: arrived(ag.at[pl.ds(0, 2), rows], pa.at[r]))
                pl.when(jnp.logical_not(mine))(lambda: arrived(ag.at[pl.ds(0, 4), rows], pa.at[r]))
            else:
                pl.when(mine)(lambda: arrived(ag.at[pl.ds(0, 3), rows], pb.at[r]))
        rows = pl.ds(128 * b, 128)
        to = pl.ds(128 * (2 * b + e), 128)
        for k, (direct, mirror) in enumerate((
            (ag[c + 2 * i, rows], ag[c + 2 * i + 4, rows]),
            (asib[i, rows], asib[i + 2, rows]),
        )):
            direct, mirror = direct.astype(jnp.float32), mirror.astype(jnp.float32)
            cols = pl.ds(512 * k, 512)
            pk[0, to, cols] = (direct + mirror).astype(jnp.bfloat16)
            pk[1, to, cols] = (direct - mirror).astype(jnp.bfloat16)

    def multiply(b, e, g):
        t = tile(b, e, g)
        rows = pl.ds(128 * (2 * b + e), 128)
        dims = (((1,), (1,)), ((), ()))
        plus = lax.dot_general(pk[0, rows], wb[g, 0], dims, preferred_element_type=jnp.float32)
        minus = lax.dot_general(pk[1, rows], wb[g, 1], dims, preferred_element_type=jnp.float32)
        cp[0, pl.ds(128 * t, 128)] = plus + minus
        cp[1, pl.ds(128 * t, 128)] = plus - minus
        target = is_target(e)
        for s in (0, 1):
            block = jnp.where(target, block_of(2), block_of(1 if s == 0 else -1))
            half = jnp.where(target, s, 1 - s)
            part = pl.ds(pl.multiple_of(128 * t + 64 * half, 64), 64)
            sx1[s, pl.ds(64 * t, 64)] = cp[block, part].astype(jnp.bfloat16)
            x1_copy(t, s).start()

    def add_on(b, e, g):
        t = tile(b, e, g)
        rows = pl.ds(64 * t, 64)
        def act():
            arrived(rx1.at[:, rows], x1r.at[t])
            for s in (0, 1):
                value = cp[block_of(1 if s == 0 else -1), pl.ds(128 * t + 64 * s, 64)]
                sx2[s, rows] = (value + rx1[s, rows].astype(jnp.float32)).astype(jnp.bfloat16)
                x2_copy(t, s).start()
        pl.when(jnp.logical_not(is_target(e)))(act)

    def finish(b, e, g):
        t = tile(b, e, g)
        rows = pl.ds(64 * t, 64)
        def act():
            arrived(rx1.at[:, rows], x1r.at[t])
            arrived(rx2.at[:, rows], x2r.at[t])
            for s in (0, 1):
                total = (
                    cp[block_of(0), pl.ds(128 * t + 64 * s, 64)]
                    + rx2[s, rows].astype(jnp.float32)
                    + rx1[1 - s, rows].astype(jnp.float32)
                ).astype(jnp.bfloat16)
                if g == 0:
                    out[pl.ds(pl.multiple_of(y * 256 + 128 * b + 64 * s, 64), 64)] = total
                else:
                    res[pl.ds(128 * (4 * b + g) + 64 * s, 64)] = total
            if g > 0:
                for h in (0, 1):
                    o_copy(b, g, h, dev(dy=owner(g, h))).start()
        pl.when(is_target(e))(act)

    def mask_own():
        for load in loads:
            load.wait()
        row_sym = row_ir[0, 0] ^ row_ir[0, 1]
        for k in (0, 1):
            keep = (row_sym == (col_ir[k, 0] ^ col_ir[k, 1])).astype(jnp.int32).astype(jnp.float32)
            cols = pl.ds(256 * k, 256)
            for s in (0, 1):
                wb[0, s, :, cols] = (wb[0, s, :, cols].astype(jnp.float32) * keep).astype(jnp.bfloat16)

    load_a.wait()
    pl.semaphore_wait(barrier, len(partners))

    def perform(steps):
        for step in steps:
            name, args = step[0], step[1:]
            if name == "zo":
                z_send(args[0], 1)
                give(args[0], 0)
            elif name == "zf":
                z_wait(*args)
                z_send(args[0], args[1] + 1)
                give(*args)
            elif name == "pk":
                pack(*args)
            elif name == "wo":
                for s in (0, 1):
                    y_copy(s, args[0]).start()
            elif name == "wk":
                mask_own()
            elif name == "wg":
                w_give(0).start()
            elif name == "wf":
                arrived(wb.at[args[0] + 1, :, :, pl.ds(0, 512)], yr.at[args[0]])
                if args[0] == 0:
                    for s in (0, 1):
                        y_copy(s, 2).start()
                w_give(args[0] + 1).start()
            elif name == "ws":
                w_give(args[0]).wait_recv()
            elif name == "mm":
                multiply(*args)
            elif name == "ra":
                add_on(*args)
            elif name == "fi":
                finish(*args)

    pl.when(mine)(lambda: perform(STEPS_MINE))
    pl.when(jnp.logical_not(mine))(lambda: perform(STEPS_OTHER))
    arrived(out.at[pl.ds(0, 768)], orr)
    left(ag.at[pl.ds(0, 7)], 0)
    pl.when(mine)(lambda: left(ag.at[pl.ds(0, 4)], 1))
    pl.when(jnp.logical_not(mine))(lambda: left(ag.at[pl.ds(0, 3)], 1))
    left(wb.at[pl.ds(0, 3), :, :, pl.ds(0, 512)], 2)
    left(wb.at[:, :, :, pl.ds(0, 512)], 3)
    left(sx1, 4)
    left(sx2.at[:, pl.ds(0, 512)], 5)
    left(res.at[pl.ds(0, 768)], 6)


STEPS_MINE = [
    ("zo", 0), ("zo", 1), ("wk",), ("wo", 0), ("zo", 2), ("wo", 1), ("zf", 0, 1), ("zf", 1, 1), ("zo", 3), ("wg",),
    ("wf", 0), ("zf", 0, 2), ("zf", 1, 2), ("zf", 2, 1), ("ws", 0), ("ws", 1), ("pk", 0, 0), ("mm", 0, 0, 1),
    ("mm", 0, 0, 0), ("zf", 0, 3), ("zf", 3, 1), ("zf", 1, 3), ("wf", 1), ("ra", 0, 0, 1), ("ra", 0, 0, 0),
    ("zf", 2, 2), ("ws", 2), ("mm", 0, 0, 2), ("zf", 3, 2), ("fi", 0, 0, 1), ("fi", 0, 0, 0), ("pk", 0, 1),
    ("mm", 0, 1, 1), ("mm", 0, 1, 2), ("wf", 2), ("zf", 2, 3), ("ra", 0, 0, 2), ("pk", 1, 0), ("mm", 1, 0, 1),
    ("mm", 1, 0, 2), ("zf", 3, 3), ("ws", 3), ("mm", 0, 0, 3), ("mm", 0, 1, 3), ("mm", 1, 0, 3), ("ra", 0, 1, 1),
    ("ra", 0, 1, 2), ("ra", 1, 0, 1), ("ra", 1, 0, 2), ("pk", 1, 1), ("mm", 1, 1, 3), ("mm", 1, 1, 1),
    ("mm", 1, 1, 2), ("fi", 0, 0, 2), ("fi", 0, 1, 1), ("fi", 0, 1, 2), ("ra", 0, 0, 3), ("ra", 0, 1, 3),
    ("ra", 1, 0, 3), ("mm", 0, 1, 0), ("ra", 1, 1, 3), ("ra", 1, 1, 1), ("ra", 1, 1, 2), ("fi", 1, 0, 1),
    ("fi", 1, 0, 2), ("mm", 1, 0, 0), ("mm", 1, 1, 0), ("fi", 0, 0, 3), ("fi", 0, 1, 3), ("fi", 1, 0, 3),
    ("fi", 1, 1, 3), ("fi", 1, 1, 1), ("fi", 1, 1, 2), ("ra", 0, 1, 0), ("ra", 1, 0, 0), ("ra", 1, 1, 0),
    ("fi", 0, 1, 0), ("fi", 1, 0, 0), ("fi", 1, 1, 0),
]

STEPS_OTHER = [
    ("zo", 0), ("zo", 1), ("wk",), ("wo", 0), ("zo", 2), ("wo", 1), ("zf", 0, 1), ("zf", 1, 1), ("zo", 3), ("wg",),
    ("wf", 0), ("zf", 0, 2), ("zf", 1, 2), ("zf", 2, 1), ("ws", 0), ("ws", 1), ("zf", 0, 3), ("zf", 3, 1),
    ("zf", 1, 3), ("wf", 1), ("zf", 2, 2), ("pk", 0, 0), ("mm", 0, 0, 1), ("mm", 0, 0, 0), ("pk", 0, 1),
    ("mm", 0, 1, 1), ("zf", 3, 2), ("mm", 0, 1, 0), ("ws", 2), ("mm", 0, 0, 2), ("mm", 0, 1, 2), ("ra", 0, 0, 1),
    ("wf", 2), ("zf", 2, 3), ("ra", 0, 0, 0), ("ra", 0, 1, 1), ("ra", 0, 1, 0), ("zf", 3, 3), ("ra", 0, 0, 2),
    ("ra", 0, 1, 2), ("ws", 3), ("mm", 0, 0, 3), ("mm", 0, 1, 3), ("pk", 1, 0), ("pk", 1, 1), ("mm", 1, 0, 3),
    ("mm", 1, 1, 3), ("fi", 0, 0, 1), ("fi", 0, 1, 1), ("mm", 1, 0, 1), ("mm", 1, 1, 1), ("ra", 0, 0, 3),
    ("ra", 0, 1, 3), ("fi", 0, 0, 2), ("fi", 0, 1, 2), ("mm", 1, 0, 2), ("mm", 1, 1, 2), ("ra", 1, 0, 3),
    ("ra", 1, 1, 3), ("fi", 0, 0, 0), ("fi", 0, 1, 0), ("fi", 0, 0, 3), ("fi", 0, 1, 3), ("ra", 1, 0, 1),
    ("ra", 1, 1, 1), ("mm", 1, 0, 0), ("mm", 1, 1, 0), ("ra", 1, 0, 2), ("ra", 1, 1, 2), ("fi", 1, 0, 3),
    ("fi", 1, 1, 3), ("fi", 1, 0, 1), ("fi", 1, 1, 1), ("ra", 1, 0, 0), ("ra", 1, 1, 0), ("fi", 1, 0, 2),
    ("fi", 1, 1, 2), ("fi", 1, 0, 0), ("fi", 1, 1, 0),
]


def on_device(amplitudes, integrals, row_irreps, col_irreps):
    count, bf16, dma = len(CHUNKS), jnp.bfloat16, pltpu.SemaphoreType.DMA
    hbm, vmem = (pl.BlockSpec(memory_space=s) for s in (pltpu.HBM, pltpu.VMEM))
    return pl.pallas_call(
        kernel,
        out_shape=jax.ShapeDtypeStruct((1024, 256), bf16),
        in_specs=[hbm] * 4,
        out_specs=vmem,
        scratch_shapes=[
            pltpu.SMEM((1, 2), jnp.int32),
            pltpu.SMEM((2, 2), jnp.int32),
            pltpu.VMEM((8, 256, 512), bf16),
            pltpu.VMEM((4, 256, 512), bf16),
            pltpu.VMEM((2, 512, 1024), bf16),
            pltpu.VMEM((4, 2, 256, 1024), bf16),
            pltpu.VMEM((2, 2048, 256), jnp.float32),
            pltpu.VMEM((2, 1024, 256), bf16),
            pltpu.VMEM((2, 1024, 256), bf16),
            pltpu.VMEM((2, 1024, 256), bf16),
            pltpu.VMEM((2, 1024, 256), bf16),
            pltpu.VMEM((1024, 256), bf16),
            dma((4,)),
            dma((7,)), dma((count, 3)), dma((count,)), dma((count,)), dma((3,)), dma((4,)), dma((16,)), dma((16,)), dma,
        ],
        compiler_params=pltpu.CompilerParams(
            collective_id=0, has_side_effects=True, vmem_limit_bytes=48 * 2**20
        ),
        cost_estimate=pl.CostEstimate(flops=2 * 2**30, bytes_accessed=2 * 2**20, transcendentals=0),
        name="ladder",
    )(*(pltpu.with_memory_space_constraint(a, pltpu.HBM) for a in (amplitudes, integrals, row_irreps, col_irreps)))


def solution(mesh):
    in_specs = (P("pair", "cd"), P(None, "pair", "cd"), P("pair", None), P("cd", None))
    out_specs = P("cd", "pair")
    return jax.shard_map(
        on_device, mesh=mesh, in_specs=in_specs, out_specs=out_specs, check_vma=False
    )
```

```python
import jax
import jax.numpy as jnp
from jax import lax
from jax.experimental import pallas as pl
from jax.experimental.pallas import tpu as pltpu
from jax.sharding import PartitionSpec as P

MESH = pl.DeviceIdType.MESH
NX, NY, NZ = 4, 4, 8

CHUNKS = (64, 64, 64, 64)


def coordinates():
    pair, cd = lax.axis_index("pair"), lax.axis_index("cd")
    return lax.div(cd, 2), lax.rem(pair, NY), lax.div(pair, NY), lax.rem(cd, 2)


def kernel(
    amp, integ, row_hbm, col_hbm, out, row_ir, col_ir,
    ag, asib, pk, wb, cp, sx1, rx1, sx2, rx2, res,
    loc, sent, zr, pa, pb, yr, wr, x1r, x2r, orr,
):
    x, y, z, c = coordinates()
    sib = 1 - c
    chunks = CHUNKS
    starts = [sum(chunks[:k]) for k in range(len(chunks))]
    def dev(dx=0, dy=0, dz=0, flip=False):
        return (
            lax.rem(z + dz + NZ, NZ) * NY + lax.rem(y + dy + NY, NY),
            lax.rem(x + dx + NX, NX) * 2 + (sib if flip else c),
        )

    load_a = pltpu.make_async_copy(amp, ag.at[z], loc.at[0])
    load_w = pltpu.make_async_copy(integ, wb.at[0, :, :, pl.ds(0, 512)], loc.at[1])
    loads = [
        load_w,
        pltpu.make_async_copy(row_hbm, row_ir, loc.at[2]),
        pltpu.make_async_copy(col_hbm, col_ir, loc.at[3]),
    ]
    load_a.start()
    for load in loads:
        load.start()
    barrier = pltpu.get_barrier_semaphore()
    partners = [
        dev(dx=1), dev(dx=-1), dev(dy=1), dev(dy=-1), dev(dy=2), dev(dz=1), dev(dz=-1), dev(flip=True),
    ]
    for partner in partners:
        pl.semaphore_signal(barrier, inc=1, device_id=partner, device_id_type=MESH)
    def remote(src, dst, send, recv, to):
        return pltpu.make_async_remote_copy(
            src_ref=src, dst_ref=dst, send_sem=send, recv_sem=recv, device_id=to, device_id_type=MESH
        )

    def arrived(ref, recv):
        remote(ref, ref, sent.at[0], recv, dev(flip=True)).wait_recv()

    def left(ref, send):
        remote(ref, ref, sent.at[send], orr, dev(flip=True)).wait_send()

    mine = lax.rem(z, 2) == c
    first = jnp.where(mine, 1 - lax.div(lax.rem(z, 4), 2), lax.div(lax.rem(z, 4), 2))

    def pair_of(e):
        return first if e == 0 else 1 - first

    def is_target(e):
        return lax.rem(x, 2) == pair_of(e)

    def z_rows(r, s, d):
        if d < 4:
            return pl.ds(starts[r], chunks[r])
        half = chunks[r] // 2
        return pl.ds(starts[r] + (0 if s == 0 else half), half)

    def z_copy(r, s, d, behind):
        sign = 1 if s == 0 else -1
        block = ag.at[lax.rem(z - sign * behind + NZ, NZ), z_rows(r, s, d)]
        return remote(block, block, sent.at[0], zr.at[r, d - 1] if d < 4 else pb.at[r], dev(dz=sign))

    def cross_copy(r, s, behind):
        sign = 1 if s == 0 else -1
        origin = lax.rem(z - sign * behind + NZ, NZ)
        rows = z_rows(r, s, 4)
        return remote(
            ag.at[origin, rows], asib.at[lax.div(origin, 2), rows], sent.at[0], pb.at[r], dev(dz=sign, flip=True)
        )

    def z_send(r, d):
        for s in (0, 1):
            copy = z_copy(r, s, d, d - 1)
            if d < 4:
                copy.start()
            else:
                pl.when(jnp.logical_not(mine))(copy.start)
                pl.when(mine)(cross_copy(r, s, 3).start)

    def z_wait(r, d):
        arrived(ag.at[pl.ds(0, 2), z_rows(r, 0, d)], zr.at[r, d - 1])

    def share(r, far):
        origin = lax.rem(z + far + NZ, NZ)
        rows = pl.ds(starts[r], chunks[r])
        return remote(
            ag.at[origin, rows], asib.at[lax.div(origin, 2), rows], sent.at[1], (pa if far else pb).at[r], dev(flip=True)
        )

    def give(r, d):
        sends = {0: (0,), 1: (1, -1), 2: (2, -2), 3: (3, -3)}[d]
        def act():
            for far in sends:
                share(r, far).start()
        pl.when(mine if d % 2 else jnp.logical_not(mine))(act)

    def y_half(s, n):
        return s if n != 1 else 1 - s

    def y_copy(s, n):
        sign = 1 if s == 0 else -1
        half = pl.ds(128 * y_half(s, n), 128)
        src = wb.at[0 if n < 2 else 1, :, half, pl.ds(0, 512)]
        dst = wb.at[n + 1, :, half, pl.ds(0, 512)]
        return remote(src, dst, sent.at[2], yr.at[n], dev(dy=sign))

    def w_give(g):
        return remote(
            wb.at[g, :, :, pl.ds(0, 512)], wb.at[g, :, :, pl.ds(512, 512)], sent.at[3], wr.at[g], dev(flip=True)
        )

    def x1_copy(t, s):
        rows = pl.ds(64 * t, 64)
        return remote(sx1.at[s, rows], rx1.at[s, rows], sent.at[4], x1r.at[t], dev(dx=1 if s == 0 else -1))

    def x2_copy(t, s):
        rows = pl.ds(64 * t, 64)
        return remote(sx2.at[s, rows], rx2.at[s, rows], sent.at[5], x2r.at[t], dev(dx=1 if s == 0 else -1))

    def owner(g, h):
        return {1: (-1, 1), 2: (1, -1), 3: (2, 2)}[g][h]

    def o_copy(b, g, h, to):
        cols = pl.ds(128 * h, 128)
        dst = out.at[pl.ds(pl.multiple_of(y * 256 + 128 * b, 128), 128), cols]
        return remote(res.at[pl.ds(128 * (4 * b + g), 128), cols], dst, sent.at[6], orr, to)

    def tile(b, e, g):
        return (2 * b + e) * 4 + g

    def block_of(dx):
        return lax.div(lax.rem(x + dx + NX, NX), 2)

    def pack(b, e):
        i = pair_of(e)
        for r in (2 * b, 2 * b + 1):
            rows = pl.ds(starts[r], chunks[r])
            if e == 0:
                pl.when(mine)(lambda: arrived(ag.at[pl.ds(0, 2), rows], pa.at[r]))
                pl.when(jnp.logical_not(mine))(lambda: arrived(ag.at[pl.ds(0, 4), rows], pa.at[r]))
            else:
                pl.when(mine)(lambda: arrived(ag.at[pl.ds(0, 3), rows], pb.at[r]))
        rows = pl.ds(128 * b, 128)
        to = pl.ds(128 * (2 * b + e), 128)
        for k, (direct, mirror) in enumerate((
            (ag[c + 2 * i, rows], ag[c + 2 * i + 4, rows]),
            (asib[i, rows], asib[i + 2, rows]),
        )):
            direct, mirror = direct.astype(jnp.float32), mirror.astype(jnp.float32)
            cols = pl.ds(512 * k, 512)
            pk[0, to, cols] = (direct + mirror).astype(jnp.bfloat16)
            pk[1, to, cols] = (direct - mirror).astype(jnp.bfloat16)

    def multiply(b, e, g):
        t = tile(b, e, g)
        rows = pl.ds(128 * (2 * b + e), 128)
        dims = (((1,), (1,)), ((), ()))
        plus = lax.dot_general(pk[0, rows], wb[g, 0], dims, preferred_element_type=jnp.float32)
        minus = lax.dot_general(pk[1, rows], wb[g, 1], dims, preferred_element_type=jnp.float32)
        cp[0, pl.ds(128 * t, 128)] = plus + minus
        cp[1, pl.ds(128 * t, 128)] = plus - minus
        target = is_target(e)
        for s in (0, 1):
            block = jnp.where(target, block_of(2), block_of(1 if s == 0 else -1))
            half = jnp.where(target, s, 1 - s)
            part = pl.ds(pl.multiple_of(128 * t + 64 * half, 64), 64)
            sx1[s, pl.ds(64 * t, 64)] = cp[block, part].astype(jnp.bfloat16)
            x1_copy(t, s).start()

    def add_on(b, e, g):
        t = tile(b, e, g)
        rows = pl.ds(64 * t, 64)
        def act():
            arrived(rx1.at[:, rows], x1r.at[t])
            for s in (0, 1):
                value = cp[block_of(1 if s == 0 else -1), pl.ds(128 * t + 64 * s, 64)]
                sx2[s, rows] = (value + rx1[s, rows].astype(jnp.float32)).astype(jnp.bfloat16)
                x2_copy(t, s).start()
        pl.when(jnp.logical_not(is_target(e)))(act)

    def finish(b, e, g):
        t = tile(b, e, g)
        rows = pl.ds(64 * t, 64)
        def act():
            arrived(rx1.at[:, rows], x1r.at[t])
            arrived(rx2.at[:, rows], x2r.at[t])
            for s in (0, 1):
                total = (
                    cp[block_of(0), pl.ds(128 * t + 64 * s, 64)]
                    + rx2[s, rows].astype(jnp.float32)
                    + rx1[1 - s, rows].astype(jnp.float32)
                ).astype(jnp.bfloat16)
                if g == 0:
                    out[pl.ds(pl.multiple_of(y * 256 + 128 * b + 64 * s, 64), 64)] = total
                else:
                    res[pl.ds(128 * (4 * b + g) + 64 * s, 64)] = total
            if g > 0:
                for h in (0, 1):
                    o_copy(b, g, h, dev(dy=owner(g, h))).start()
        pl.when(is_target(e))(act)

    def mask_own():
        for load in loads:
            load.wait()
        row_sym = row_ir[0, 0] ^ row_ir[0, 1]
        for k in (0, 1):
            keep = (row_sym == (col_ir[k, 0] ^ col_ir[k, 1])).astype(jnp.int32).astype(jnp.float32)
            cols = pl.ds(256 * k, 256)
            for s in (0, 1):
                wb[0, s, :, cols] = (wb[0, s, :, cols].astype(jnp.float32) * keep).astype(jnp.bfloat16)

    load_a.wait()
    pl.semaphore_wait(barrier, len(partners))

    def perform(steps):
        for step in steps:
            name, args = step[0], step[1:]
            if name == "zo":
                z_send(args[0], 1)
                give(args[0], 0)
            elif name == "zf":
                z_wait(*args)
                z_send(args[0], args[1] + 1)
                give(*args)
            elif name == "pk":
                pack(*args)
            elif name == "wo":
                for s in (0, 1):
                    y_copy(s, args[0]).start()
            elif name == "wk":
                mask_own()
            elif name == "wg":
                w_give(0).start()
            elif name == "wf":
                arrived(wb.at[args[0] + 1, :, :, pl.ds(0, 512)], yr.at[args[0]])
                if args[0] == 0:
                    for s in (0, 1):
                        y_copy(s, 2).start()
                w_give(args[0] + 1).start()
            elif name == "ws":
                w_give(args[0]).wait_recv()
            elif name == "mm":
                multiply(*args)
            elif name == "ra":
                add_on(*args)
            elif name == "fi":
                finish(*args)

    pl.when(mine)(lambda: perform(STEPS_MINE))
    pl.when(jnp.logical_not(mine))(lambda: perform(STEPS_OTHER))
    arrived(out.at[pl.ds(0, 768)], orr)
    left(ag.at[pl.ds(0, 7)], 0)
    pl.when(mine)(lambda: left(ag.at[pl.ds(0, 4)], 1))
    pl.when(jnp.logical_not(mine))(lambda: left(ag.at[pl.ds(0, 3)], 1))
    left(wb.at[pl.ds(0, 3), :, :, pl.ds(0, 512)], 2)
    left(wb.at[:, :, :, pl.ds(0, 512)], 3)
    left(sx1, 4)
    left(sx2.at[:, pl.ds(0, 512)], 5)
    left(res.at[pl.ds(0, 768)], 6)


STEPS_MINE = [
    ("zo", 0), ("zo", 1), ("wk",), ("wo", 0), ("zo", 2), ("wo", 1), ("zf", 0, 1), ("zf", 1, 1), ("zo", 3), ("wg",),
    ("wf", 0), ("zf", 0, 2), ("zf", 1, 2), ("zf", 2, 1), ("ws", 0), ("ws", 1), ("pk", 0, 0), ("mm", 0, 0, 1),
    ("mm", 0, 0, 0), ("zf", 0, 3), ("zf", 3, 1), ("zf", 1, 3), ("wf", 1), ("ra", 0, 0, 1), ("ra", 0, 0, 0),
    ("zf", 2, 2), ("ws", 2), ("mm", 0, 0, 2), ("zf", 3, 2), ("fi", 0, 0, 1), ("fi", 0, 0, 0), ("pk", 0, 1),
    ("mm", 0, 1, 1), ("mm", 0, 1, 2), ("wf", 2), ("zf", 2, 3), ("ra", 0, 0, 2), ("pk", 1, 0), ("mm", 1, 0, 1),
    ("mm", 1, 0, 2), ("zf", 3, 3), ("ws", 3), ("mm", 0, 0, 3), ("mm", 0, 1, 3), ("mm", 1, 0, 3), ("ra", 0, 1, 1),
    ("ra", 0, 1, 2), ("ra", 1, 0, 1), ("ra", 1, 0, 2), ("pk", 1, 1), ("mm", 1, 1, 3), ("mm", 1, 1, 1),
    ("mm", 1, 1, 2), ("fi", 0, 0, 2), ("fi", 0, 1, 1), ("fi", 0, 1, 2), ("ra", 0, 0, 3), ("ra", 0, 1, 3),
    ("ra", 1, 0, 3), ("mm", 0, 1, 0), ("ra", 1, 1, 3), ("ra", 1, 1, 1), ("ra", 1, 1, 2), ("fi", 1, 0, 1),
    ("fi", 1, 0, 2), ("mm", 1, 0, 0), ("mm", 1, 1, 0), ("fi", 0, 0, 3), ("fi", 0, 1, 3), ("fi", 1, 0, 3),
    ("fi", 1, 1, 3), ("fi", 1, 1, 1), ("fi", 1, 1, 2), ("ra", 0, 1, 0), ("ra", 1, 0, 0), ("ra", 1, 1, 0),
    ("fi", 0, 1, 0), ("fi", 1, 0, 0), ("fi", 1, 1, 0),
]

STEPS_OTHER = [
    ("zo", 0), ("zo", 1), ("wk",), ("wo", 0), ("zo", 2), ("wo", 1), ("zf", 0, 1), ("zf", 1, 1), ("zo", 3), ("wg",),
    ("wf", 0), ("zf", 0, 2), ("zf", 1, 2), ("zf", 2, 1), ("ws", 0), ("ws", 1), ("zf", 0, 3), ("zf", 3, 1),
    ("zf", 1, 3), ("wf", 1), ("zf", 2, 2), ("pk", 0, 0), ("mm", 0, 0, 1), ("mm", 0, 0, 0), ("pk", 0, 1),
    ("mm", 0, 1, 1), ("zf", 3, 2), ("mm", 0, 1, 0), ("ws", 2), ("mm", 0, 0, 2), ("mm", 0, 1, 2), ("ra", 0, 0, 1),
    ("wf", 2), ("zf", 2, 3), ("ra", 0, 0, 0), ("ra", 0, 1, 1), ("ra", 0, 1, 0), ("zf", 3, 3), ("ra", 0, 0, 2),
    ("ra", 0, 1, 2), ("ws", 3), ("mm", 0, 0, 3), ("mm", 0, 1, 3), ("pk", 1, 0), ("pk", 1, 1), ("mm", 1, 0, 3),
    ("mm", 1, 1, 3), ("mm", 1, 0, 1), ("mm", 1, 1, 1), ("mm", 1, 0, 2), ("mm", 1, 1, 2), ("fi", 0, 0, 1),
    ("fi", 0, 1, 1), ("ra", 0, 0, 3), ("ra", 0, 1, 3), ("fi", 0, 0, 2), ("fi", 0, 1, 2), ("ra", 1, 0, 3),
    ("ra", 1, 1, 3), ("fi", 0, 0, 0), ("fi", 0, 1, 0), ("ra", 1, 0, 1), ("ra", 1, 1, 1), ("mm", 1, 0, 0),
    ("mm", 1, 1, 0), ("fi", 0, 0, 3), ("fi", 0, 1, 3), ("ra", 1, 0, 2), ("ra", 1, 1, 2), ("fi", 1, 0, 3),
    ("fi", 1, 1, 3), ("fi", 1, 0, 1), ("fi", 1, 1, 1), ("ra", 1, 0, 0), ("ra", 1, 1, 0), ("fi", 1, 0, 2),
    ("fi", 1, 1, 2), ("fi", 1, 0, 0), ("fi", 1, 1, 0),
]


def on_device(amplitudes, integrals, row_irreps, col_irreps):
    count, bf16, dma = len(CHUNKS), jnp.bfloat16, pltpu.SemaphoreType.DMA
    hbm, vmem = (pl.BlockSpec(memory_space=s) for s in (pltpu.HBM, pltpu.VMEM))
    return pl.pallas_call(
        kernel,
        out_shape=jax.ShapeDtypeStruct((1024, 256), bf16),
        in_specs=[hbm] * 4,
        out_specs=vmem,
        scratch_shapes=[
            pltpu.SMEM((1, 2), jnp.int32),
            pltpu.SMEM((2, 2), jnp.int32),
            pltpu.VMEM((8, 256, 512), bf16),
            pltpu.VMEM((4, 256, 512), bf16),
            pltpu.VMEM((2, 512, 1024), bf16),
            pltpu.VMEM((4, 2, 256, 1024), bf16),
            pltpu.VMEM((2, 2048, 256), jnp.float32),
            pltpu.VMEM((2, 1024, 256), bf16),
            pltpu.VMEM((2, 1024, 256), bf16),
            pltpu.VMEM((2, 1024, 256), bf16),
            pltpu.VMEM((2, 1024, 256), bf16),
            pltpu.VMEM((1024, 256), bf16),
            dma((4,)),
            dma((7,)), dma((count, 3)), dma((count,)), dma((count,)), dma((3,)), dma((4,)), dma((16,)), dma((16,)), dma,
        ],
        compiler_params=pltpu.CompilerParams(
            collective_id=0, has_side_effects=True, vmem_limit_bytes=48 * 2**20
        ),
        cost_estimate=pl.CostEstimate(flops=2 * 2**30, bytes_accessed=2 * 2**20, transcendentals=0),
        name="ladder",
    )(*(pltpu.with_memory_space_constraint(a, pltpu.HBM) for a in (amplitudes, integrals, row_irreps, col_irreps)))


def solution(mesh):
    in_specs = (P("pair", "cd"), P(None, "pair", "cd"), P("pair", None), P("cd", None))
    out_specs = P("cd", "pair")
    return jax.shard_map(
        on_device, mesh=mesh, in_specs=in_specs, out_specs=out_specs, check_vma=False
    )
```

```python
import jax
import jax.numpy as jnp
from jax import lax
from jax.experimental import pallas as pl
from jax.experimental.pallas import tpu as pltpu
from jax.sharding import PartitionSpec as P

MESH = pl.DeviceIdType.MESH
NX, NY, NZ = 4, 4, 8

CHUNKS = (64, 64, 64, 64)


def coordinates():
    pair, cd = lax.axis_index("pair"), lax.axis_index("cd")
    return lax.div(cd, 2), lax.rem(pair, NY), lax.div(pair, NY), lax.rem(cd, 2)


def kernel(
    amp, integ, row_hbm, col_hbm, out, row_ir, col_ir,
    ag, asib, pk, wb, cp, sx1, rx1, sx2, rx2, res,
    loc, sent, zr, pa, pb, yr, wr, x1r, x2r, orr,
):
    x, y, z, c = coordinates()
    sib = 1 - c
    chunks = CHUNKS
    starts = [sum(chunks[:k]) for k in range(len(chunks))]
    def dev(dx=0, dy=0, dz=0, flip=False):
        return (
            lax.rem(z + dz + NZ, NZ) * NY + lax.rem(y + dy + NY, NY),
            lax.rem(x + dx + NX, NX) * 2 + (sib if flip else c),
        )

    load_a = pltpu.make_async_copy(amp, ag.at[z], loc.at[0])
    load_w = pltpu.make_async_copy(integ, wb.at[0, :, :, pl.ds(0, 512)], loc.at[1])
    loads = [
        load_w, load_a,
        pltpu.make_async_copy(row_hbm, row_ir, loc.at[2]),
        pltpu.make_async_copy(col_hbm, col_ir, loc.at[3]),
    ]
    for load in loads:
        load.start()
    barrier = pltpu.get_barrier_semaphore()
    partners = [
        dev(dx=1), dev(dx=-1), dev(dy=1), dev(dy=-1), dev(dy=2), dev(dz=1), dev(dz=-1), dev(flip=True),
    ]
    for partner in partners:
        pl.semaphore_signal(barrier, inc=1, device_id=partner, device_id_type=MESH)
    def remote(src, dst, send, recv, to):
        return pltpu.make_async_remote_copy(
            src_ref=src, dst_ref=dst, send_sem=send, recv_sem=recv, device_id=to, device_id_type=MESH
        )

    def arrived(ref, recv):
        remote(ref, ref, sent.at[0], recv, dev(flip=True)).wait_recv()

    def left(ref, send):
        remote(ref, ref, sent.at[send], orr, dev(flip=True)).wait_send()

    mine = lax.rem(z, 2) == c
    first = jnp.where(mine, 1 - lax.div(lax.rem(z, 4), 2), lax.div(lax.rem(z, 4), 2))

    def pair_of(e):
        return first if e == 0 else 1 - first

    def is_target(e):
        return lax.rem(x, 2) == pair_of(e)

    def z_rows(r, s, d):
        if d < 4:
            return pl.ds(starts[r], chunks[r])
        half = chunks[r] // 2
        return pl.ds(starts[r] + (0 if s == 0 else half), half)

    def z_copy(r, s, d, behind):
        sign = 1 if s == 0 else -1
        block = ag.at[lax.rem(z - sign * behind + NZ, NZ), z_rows(r, s, d)]
        src = amp.at[z_rows(r, s, d)] if d == 1 else block
        return remote(src, block, sent.at[0], zr.at[r, d - 1] if d < 4 else pb.at[r], dev(dz=sign))

    def cross_copy(r, s, behind):
        sign = 1 if s == 0 else -1
        origin = lax.rem(z - sign * behind + NZ, NZ)
        rows = z_rows(r, s, 4)
        return remote(
            ag.at[origin, rows], asib.at[lax.div(origin, 2), rows], sent.at[0], pb.at[r], dev(dz=sign, flip=True)
        )

    def z_send(r, d):
        for s in (0, 1):
            copy = z_copy(r, s, d, d - 1)
            if d < 4:
                copy.start()
            else:
                pl.when(jnp.logical_not(mine))(copy.start)
                pl.when(mine)(cross_copy(r, s, 3).start)

    def z_wait(r, d):
        arrived(ag.at[pl.ds(0, 2), z_rows(r, 0, d)], zr.at[r, d - 1])

    def share(r, far):
        origin = lax.rem(z + far + NZ, NZ)
        rows = pl.ds(starts[r], chunks[r])
        return remote(
            ag.at[origin, rows] if far else amp.at[rows], asib.at[lax.div(origin, 2), rows], sent.at[1], (pa if far else pb).at[r], dev(flip=True)
        )

    def give(r, d):
        sends = {0: (0,), 1: (1, -1), 2: (2, -2), 3: (3, -3)}[d]
        def act():
            for far in sends:
                share(r, far).start()
        pl.when(mine if d % 2 else jnp.logical_not(mine))(act)

    def y_half(s, n):
        return s if n != 1 else 1 - s

    def y_copy(s, n):
        sign = 1 if s == 0 else -1
        half = pl.ds(128 * y_half(s, n), 128)
        src = wb.at[0 if n < 2 else 1, :, half, pl.ds(0, 512)]
        dst = wb.at[n + 1, :, half, pl.ds(0, 512)]
        return remote(src, dst, sent.at[2], yr.at[n], dev(dy=sign))

    def w_give(g):
        return remote(
            wb.at[g, :, :, pl.ds(0, 512)], wb.at[g, :, :, pl.ds(512, 512)], sent.at[3], wr.at[g], dev(flip=True)
        )

    def x1_copy(t, s):
        rows = pl.ds(64 * t, 64)
        return remote(sx1.at[s, rows], rx1.at[s, rows], sent.at[4], x1r.at[t], dev(dx=1 if s == 0 else -1))

    def x2_copy(t, s):
        rows = pl.ds(64 * t, 64)
        return remote(sx2.at[s, rows], rx2.at[s, rows], sent.at[5], x2r.at[t], dev(dx=1 if s == 0 else -1))

    def owner(g, h):
        return {1: (-1, 1), 2: (1, -1), 3: (2, 2)}[g][h]

    def o_copy(b, g, h, to):
        cols = pl.ds(128 * h, 128)
        dst = out.at[pl.ds(pl.multiple_of(y * 256 + 128 * b, 128), 128), cols]
        return remote(res.at[pl.ds(128 * (4 * b + g), 128), cols], dst, sent.at[6], orr, to)

    def tile(b, e, g):
        return (2 * b + e) * 4 + g

    def block_of(dx):
        return lax.div(lax.rem(x + dx + NX, NX), 2)

    def pack(b, e):
        i = pair_of(e)
        for r in (2 * b, 2 * b + 1):
            rows = pl.ds(starts[r], chunks[r])
            if e == 0:
                pl.when(mine)(lambda: arrived(ag.at[pl.ds(0, 2), rows], pa.at[r]))
                pl.when(jnp.logical_not(mine))(lambda: arrived(ag.at[pl.ds(0, 4), rows], pa.at[r]))
            else:
                pl.when(mine)(lambda: arrived(ag.at[pl.ds(0, 3), rows], pb.at[r]))
        rows = pl.ds(128 * b, 128)
        to = pl.ds(128 * (2 * b + e), 128)
        for k, (direct, mirror) in enumerate((
            (ag[c + 2 * i, rows], ag[c + 2 * i + 4, rows]),
            (asib[i, rows], asib[i + 2, rows]),
        )):
            direct, mirror = direct.astype(jnp.float32), mirror.astype(jnp.float32)
            cols = pl.ds(512 * k, 512)
            pk[0, to, cols] = (direct + mirror).astype(jnp.bfloat16)
            pk[1, to, cols] = (direct - mirror).astype(jnp.bfloat16)

    def multiply(b, e, g):
        t = tile(b, e, g)
        rows = pl.ds(128 * (2 * b + e), 128)
        dims = (((1,), (1,)), ((), ()))
        plus = lax.dot_general(pk[0, rows], wb[g, 0], dims, preferred_element_type=jnp.float32)
        minus = lax.dot_general(pk[1, rows], wb[g, 1], dims, preferred_element_type=jnp.float32)
        cp[0, pl.ds(128 * t, 128)] = plus + minus
        cp[1, pl.ds(128 * t, 128)] = plus - minus
        target = is_target(e)
        for s in (0, 1):
            block = jnp.where(target, block_of(2), block_of(1 if s == 0 else -1))
            half = jnp.where(target, s, 1 - s)
            part = pl.ds(pl.multiple_of(128 * t + 64 * half, 64), 64)
            sx1[s, pl.ds(64 * t, 64)] = cp[block, part].astype(jnp.bfloat16)
            x1_copy(t, s).start()

    def add_on(b, e, g):
        t = tile(b, e, g)
        rows = pl.ds(64 * t, 64)
        def act():
            arrived(rx1.at[:, rows], x1r.at[t])
            for s in (0, 1):
                value = cp[block_of(1 if s == 0 else -1), pl.ds(128 * t + 64 * s, 64)]
                sx2[s, rows] = (value + rx1[s, rows].astype(jnp.float32)).astype(jnp.bfloat16)
                x2_copy(t, s).start()
        pl.when(jnp.logical_not(is_target(e)))(act)

    def finish(b, e, g):
        t = tile(b, e, g)
        rows = pl.ds(64 * t, 64)
        def act():
            arrived(rx1.at[:, rows], x1r.at[t])
            arrived(rx2.at[:, rows], x2r.at[t])
            for s in (0, 1):
                total = (
                    cp[block_of(0), pl.ds(128 * t + 64 * s, 64)]
                    + rx2[s, rows].astype(jnp.float32)
                    + rx1[1 - s, rows].astype(jnp.float32)
                ).astype(jnp.bfloat16)
                if g == 0:
                    out[pl.ds(pl.multiple_of(y * 256 + 128 * b + 64 * s, 64), 64)] = total
                else:
                    res[pl.ds(128 * (4 * b + g) + 64 * s, 64)] = total
            if g > 0:
                for h in (0, 1):
                    o_copy(b, g, h, dev(dy=owner(g, h))).start()
        pl.when(is_target(e))(act)

    def mask_own():
        for load in loads:
            load.wait()
        row_sym = row_ir[0, 0] ^ row_ir[0, 1]
        for k in (0, 1):
            keep = (row_sym == (col_ir[k, 0] ^ col_ir[k, 1])).astype(jnp.int32).astype(jnp.float32)
            cols = pl.ds(256 * k, 256)
            for s in (0, 1):
                wb[0, s, :, cols] = (wb[0, s, :, cols].astype(jnp.float32) * keep).astype(jnp.bfloat16)

    pl.semaphore_wait(barrier, len(partners))

    def perform(steps):
        for step in steps:
            name, args = step[0], step[1:]
            if name == "zo":
                z_send(args[0], 1)
                give(args[0], 0)
            elif name == "zf":
                z_wait(*args)
                z_send(args[0], args[1] + 1)
                give(*args)
            elif name == "pk":
                pack(*args)
            elif name == "wo":
                for s in (0, 1):
                    y_copy(s, args[0]).start()
            elif name == "wk":
                mask_own()
            elif name == "wg":
                w_give(0).start()
            elif name == "wf":
                arrived(wb.at[args[0] + 1, :, :, pl.ds(0, 512)], yr.at[args[0]])
                if args[0] == 0:
                    for s in (0, 1):
                        y_copy(s, 2).start()
                w_give(args[0] + 1).start()
            elif name == "ws":
                w_give(args[0]).wait_recv()
            elif name == "mm":
                multiply(*args)
            elif name == "ra":
                add_on(*args)
            elif name == "fi":
                finish(*args)

    pl.when(mine)(lambda: perform(STEPS_MINE))
    pl.when(jnp.logical_not(mine))(lambda: perform(STEPS_OTHER))
    arrived(out.at[pl.ds(0, 768)], orr)
    left(ag.at[pl.ds(0, 7)], 0)
    pl.when(mine)(lambda: left(ag.at[pl.ds(0, 4)], 1))
    pl.when(jnp.logical_not(mine))(lambda: left(ag.at[pl.ds(0, 3)], 1))
    left(wb.at[pl.ds(0, 3), :, :, pl.ds(0, 512)], 2)
    left(wb.at[:, :, :, pl.ds(0, 512)], 3)
    left(sx1, 4)
    left(sx2.at[:, pl.ds(0, 512)], 5)
    left(res.at[pl.ds(0, 768)], 6)


STEPS_MINE = [
    ("zo", 0), ("zo", 1), ("wk",), ("wo", 0), ("zo", 2), ("wo", 1), ("zf", 0, 1), ("zf", 1, 1), ("zo", 3), ("wg",),
    ("wf", 0), ("zf", 0, 2), ("zf", 1, 2), ("zf", 2, 1), ("ws", 0), ("ws", 1), ("pk", 0, 0), ("mm", 0, 0, 1),
    ("mm", 0, 0, 0), ("zf", 0, 3), ("zf", 3, 1), ("zf", 1, 3), ("wf", 1), ("ra", 0, 0, 1), ("ra", 0, 0, 0),
    ("zf", 2, 2), ("ws", 2), ("mm", 0, 0, 2), ("zf", 3, 2), ("fi", 0, 0, 1), ("fi", 0, 0, 0), ("pk", 0, 1),
    ("mm", 0, 1, 1), ("mm", 0, 1, 2), ("wf", 2), ("zf", 2, 3), ("ra", 0, 0, 2), ("pk", 1, 0), ("mm", 1, 0, 1),
    ("mm", 1, 0, 2), ("zf", 3, 3), ("ws", 3), ("mm", 0, 0, 3), ("mm", 0, 1, 3), ("mm", 1, 0, 3), ("ra", 0, 1, 1),
    ("ra", 0, 1, 2), ("ra", 1, 0, 1), ("ra", 1, 0, 2), ("pk", 1, 1), ("mm", 1, 1, 3), ("mm", 1, 1, 1),
    ("mm", 1, 1, 2), ("fi", 0, 0, 2), ("fi", 0, 1, 1), ("fi", 0, 1, 2), ("ra", 0, 0, 3), ("ra", 0, 1, 3),
    ("ra", 1, 0, 3), ("mm", 0, 1, 0), ("ra", 1, 1, 3), ("ra", 1, 1, 1), ("ra", 1, 1, 2), ("fi", 1, 0, 1),
    ("fi", 1, 0, 2), ("mm", 1, 0, 0), ("mm", 1, 1, 0), ("fi", 0, 0, 3), ("fi", 0, 1, 3), ("fi", 1, 0, 3),
    ("fi", 1, 1, 3), ("fi", 1, 1, 1), ("fi", 1, 1, 2), ("ra", 0, 1, 0), ("ra", 1, 0, 0), ("ra", 1, 1, 0),
    ("fi", 0, 1, 0), ("fi", 1, 0, 0), ("fi", 1, 1, 0),
]

STEPS_OTHER = [
    ("zo", 0), ("zo", 1), ("wk",), ("wo", 0), ("zo", 2), ("wo", 1), ("zf", 0, 1), ("zf", 1, 1), ("zo", 3), ("wg",),
    ("wf", 0), ("zf", 0, 2), ("zf", 1, 2), ("zf", 2, 1), ("ws", 0), ("ws", 1), ("zf", 0, 3), ("zf", 3, 1),
    ("zf", 1, 3), ("wf", 1), ("zf", 2, 2), ("pk", 0, 0), ("mm", 0, 0, 1), ("mm", 0, 0, 0), ("pk", 0, 1),
    ("mm", 0, 1, 1), ("zf", 3, 2), ("mm", 0, 1, 0), ("ws", 2), ("mm", 0, 0, 2), ("mm", 0, 1, 2), ("ra", 0, 0, 1),
    ("wf", 2), ("zf", 2, 3), ("ra", 0, 0, 0), ("ra", 0, 1, 1), ("ra", 0, 1, 0), ("zf", 3, 3), ("ws", 3),
    ("mm", 0, 0, 3), ("mm", 0, 1, 3), ("ra", 0, 0, 2), ("ra", 0, 1, 2), ("pk", 1, 0), ("pk", 1, 1), ("mm", 1, 0, 3),
    ("mm", 1, 1, 3), ("mm", 1, 0, 1), ("mm", 1, 1, 1), ("mm", 1, 0, 2), ("mm", 1, 1, 2), ("fi", 0, 0, 1),
    ("fi", 0, 1, 1), ("ra", 0, 0, 3), ("ra", 0, 1, 3), ("fi", 0, 0, 2), ("fi", 0, 1, 2), ("ra", 1, 0, 3),
    ("ra", 1, 1, 3), ("fi", 0, 0, 0), ("fi", 0, 1, 0), ("ra", 1, 0, 1), ("ra", 1, 1, 1), ("mm", 1, 0, 0),
    ("mm", 1, 1, 0), ("fi", 0, 0, 3), ("fi", 0, 1, 3), ("ra", 1, 0, 2), ("ra", 1, 1, 2), ("fi", 1, 0, 3),
    ("fi", 1, 1, 3), ("fi", 1, 0, 1), ("fi", 1, 1, 1), ("ra", 1, 0, 0), ("ra", 1, 1, 0), ("fi", 1, 0, 2),
    ("fi", 1, 1, 2), ("fi", 1, 0, 0), ("fi", 1, 1, 0),
]


def on_device(amplitudes, integrals, row_irreps, col_irreps):
    count, bf16, dma = len(CHUNKS), jnp.bfloat16, pltpu.SemaphoreType.DMA
    hbm, vmem = (pl.BlockSpec(memory_space=s) for s in (pltpu.HBM, pltpu.VMEM))
    return pl.pallas_call(
        kernel,
        out_shape=jax.ShapeDtypeStruct((1024, 256), bf16),
        in_specs=[hbm] * 4,
        out_specs=vmem,
        scratch_shapes=[
            pltpu.SMEM((1, 2), jnp.int32),
            pltpu.SMEM((2, 2), jnp.int32),
            pltpu.VMEM((8, 256, 512), bf16),
            pltpu.VMEM((4, 256, 512), bf16),
            pltpu.VMEM((2, 512, 1024), bf16),
            pltpu.VMEM((4, 2, 256, 1024), bf16),
            pltpu.VMEM((2, 2048, 256), jnp.float32),
            pltpu.VMEM((2, 1024, 256), bf16),
            pltpu.VMEM((2, 1024, 256), bf16),
            pltpu.VMEM((2, 1024, 256), bf16),
            pltpu.VMEM((2, 1024, 256), bf16),
            pltpu.VMEM((1024, 256), bf16),
            dma((4,)),
            dma((7,)), dma((count, 3)), dma((count,)), dma((count,)), dma((3,)), dma((4,)), dma((16,)), dma((16,)), dma,
        ],
        compiler_params=pltpu.CompilerParams(
            collective_id=0, has_side_effects=True, vmem_limit_bytes=48 * 2**20
        ),
        cost_estimate=pl.CostEstimate(flops=2 * 2**30, bytes_accessed=2 * 2**20, transcendentals=0),
        name="ladder",
    )(*(pltpu.with_memory_space_constraint(a, pltpu.HBM) for a in (amplitudes, integrals, row_irreps, col_irreps)))


def solution(mesh):
    in_specs = (P("pair", "cd"), P(None, "pair", "cd"), P("pair", None), P("cd", None))
    out_specs = P("cd", "pair")
    return jax.shard_map(
        on_device, mesh=mesh, in_specs=in_specs, out_specs=out_specs, check_vma=False
    )
```

```python
import jax
import jax.numpy as jnp
from jax import lax
from jax.experimental import pallas as pl
from jax.experimental.pallas import tpu as pltpu
from jax.sharding import PartitionSpec as P

MESH = pl.DeviceIdType.MESH
NX, NY, NZ = 4, 4, 8

CHUNKS = (64, 64, 64, 64)


def coordinates():
    pair, cd = lax.axis_index("pair"), lax.axis_index("cd")
    return lax.div(cd, 2), lax.rem(pair, NY), lax.div(pair, NY), lax.rem(cd, 2)


def kernel(
    amp, integ, row_hbm, col_hbm, out, row_ir, col_ir,
    ag, asib, pk, wb, cp, sx1, rx1, sx2, rx2, res,
    loc, sent, zr, pa, pb, yr, wr, x1r, x2r, orr,
):
    x, y, z, c = coordinates()
    sib = 1 - c
    chunks = CHUNKS
    starts = [sum(chunks[:k]) for k in range(len(chunks))]
    def dev(dx=0, dy=0, dz=0, flip=False):
        return (
            lax.rem(z + dz + NZ, NZ) * NY + lax.rem(y + dy + NY, NY),
            lax.rem(x + dx + NX, NX) * 2 + (sib if flip else c),
        )

    load_a = pltpu.make_async_copy(amp, ag.at[z], loc.at[0])
    load_w = pltpu.make_async_copy(integ, wb.at[0, :, :, pl.ds(0, 512)], loc.at[1])
    loads = [
        load_w,
        pltpu.make_async_copy(row_hbm, row_ir, loc.at[2]),
        pltpu.make_async_copy(col_hbm, col_ir, loc.at[3]),
    ]
    load_a.start()
    for load in loads:
        load.start()
    barrier = pltpu.get_barrier_semaphore()
    partners = [
        dev(dx=1), dev(dx=-1), dev(dy=1), dev(dy=-1), dev(dy=2), dev(dz=1), dev(dz=-1), dev(flip=True),
    ]
    for partner in partners:
        pl.semaphore_signal(barrier, inc=1, device_id=partner, device_id_type=MESH)
    def remote(src, dst, send, recv, to):
        return pltpu.make_async_remote_copy(
            src_ref=src, dst_ref=dst, send_sem=send, recv_sem=recv, device_id=to, device_id_type=MESH
        )

    def arrived(ref, recv):
        remote(ref, ref, sent.at[0], recv, dev(flip=True)).wait_recv()

    def left(ref, send):
        remote(ref, ref, sent.at[send], orr, dev(flip=True)).wait_send()

    mine = lax.rem(z, 2) == c
    first = jnp.where(mine, 1 - lax.div(lax.rem(z, 4), 2), lax.div(lax.rem(z, 4), 2))

    def pair_of(e):
        return first if e == 0 else 1 - first

    def is_target(e):
        return lax.rem(x, 2) == pair_of(e)

    def z_rows(r, s, d):
        if d < 4:
            return pl.ds(starts[r], chunks[r])
        half = chunks[r] // 2
        return pl.ds(starts[r] + (0 if s == 0 else half), half)

    def z_copy(r, s, d, behind):
        sign = 1 if s == 0 else -1
        block = ag.at[lax.rem(z - sign * behind + NZ, NZ), z_rows(r, s, d)]
        return remote(block, block, sent.at[0], zr.at[r, d - 1] if d < 4 else pb.at[r], dev(dz=sign))

    def cross_copy(r, s, behind):
        sign = 1 if s == 0 else -1
        origin = lax.rem(z - sign * behind + NZ, NZ)
        rows = z_rows(r, s, 4)
        return remote(
            ag.at[origin, rows], asib.at[lax.div(origin, 2), rows], sent.at[0], pb.at[r], dev(dz=sign, flip=True)
        )

    def z_send(r, d):
        for s in (0, 1):
            copy = z_copy(r, s, d, d - 1)
            if d < 4:
                copy.start()
            else:
                pl.when(jnp.logical_not(mine))(copy.start)
                pl.when(mine)(cross_copy(r, s, 3).start)

    def z_wait(r, d):
        arrived(ag.at[pl.ds(0, 2), z_rows(r, 0, d)], zr.at[r, d - 1])

    def share(r, far):
        origin = lax.rem(z + far + NZ, NZ)
        rows = pl.ds(starts[r], chunks[r])
        return remote(
            ag.at[origin, rows], asib.at[lax.div(origin, 2), rows], sent.at[1], (pa if far else pb).at[r], dev(flip=True)
        )

    def give(r, d):
        sends = {0: (0,), 1: (1, -1), 2: (2, -2), 3: (3, -3)}[d]
        def act():
            for far in sends:
                share(r, far).start()
        pl.when(mine if d % 2 else jnp.logical_not(mine))(act)

    def y_half(s, n):
        return s if n != 1 else 1 - s

    def y_copy(s, n):
        sign = 1 if s == 0 else -1
        half = pl.ds(128 * y_half(s, n), 128)
        src = wb.at[0 if n < 2 else 1, :, half, pl.ds(0, 512)]
        dst = wb.at[n + 1, :, half, pl.ds(0, 512)]
        return remote(src, dst, sent.at[2], yr.at[n], dev(dy=sign))

    def w_give(g):
        return remote(
            wb.at[g, :, :, pl.ds(0, 512)], wb.at[g, :, :, pl.ds(512, 512)], sent.at[3], wr.at[g], dev(flip=True)
        )

    def x1_copy(t, s):
        rows = pl.ds(64 * t, 64)
        return remote(sx1.at[s, rows], rx1.at[s, rows], sent.at[4], x1r.at[t], dev(dx=1 if s == 0 else -1))

    def x2_copy(t, s):
        rows = pl.ds(64 * t, 64)
        return remote(sx2.at[s, rows], rx2.at[s, rows], sent.at[5], x2r.at[t], dev(dx=1 if s == 0 else -1))

    def owner(g, h):
        return {1: (-1, 1), 2: (1, -1), 3: (2, 2)}[g][h]

    def o_copy(b, g, h, to):
        cols = pl.ds(128 * h, 128) if g < 3 else pl.ds(0, 256)
        dst = out.at[pl.ds(pl.multiple_of(y * 256 + 128 * b, 128), 128), cols]
        return remote(res.at[pl.ds(128 * (4 * b + g), 128), cols], dst, sent.at[6], orr, to)

    def tile(b, e, g):
        return (2 * b + e) * 4 + g

    def block_of(dx):
        return lax.div(lax.rem(x + dx + NX, NX), 2)

    def pack(b, e):
        i = pair_of(e)
        for r in (2 * b, 2 * b + 1):
            rows = pl.ds(starts[r], chunks[r])
            if e == 0:
                pl.when(mine)(lambda: arrived(ag.at[pl.ds(0, 2), rows], pa.at[r]))
                pl.when(jnp.logical_not(mine))(lambda: arrived(ag.at[pl.ds(0, 4), rows], pa.at[r]))
            else:
                pl.when(mine)(lambda: arrived(ag.at[pl.ds(0, 3), rows], pb.at[r]))
        rows = pl.ds(128 * b, 128)
        to = pl.ds(128 * (2 * b + e), 128)
        for k, (direct, mirror) in enumerate((
            (ag[c + 2 * i, rows], ag[c + 2 * i + 4, rows]),
            (asib[i, rows], asib[i + 2, rows]),
        )):
            direct, mirror = direct.astype(jnp.float32), mirror.astype(jnp.float32)
            cols = pl.ds(512 * k, 512)
            pk[0, to, cols] = (direct + mirror).astype(jnp.bfloat16)
            pk[1, to, cols] = (direct - mirror).astype(jnp.bfloat16)

    def multiply(b, e, g):
        t = tile(b, e, g)
        rows = pl.ds(128 * (2 * b + e), 128)
        dims = (((1,), (1,)), ((), ()))
        plus = lax.dot_general(pk[0, rows], wb[g, 0], dims, preferred_element_type=jnp.float32)
        minus = lax.dot_general(pk[1, rows], wb[g, 1], dims, preferred_element_type=jnp.float32)
        cp[0, pl.ds(128 * t, 128)] = plus + minus
        cp[1, pl.ds(128 * t, 128)] = plus - minus
        target = is_target(e)
        for s in (0, 1):
            block = jnp.where(target, block_of(2), block_of(1 if s == 0 else -1))
            half = jnp.where(target, s, 1 - s)
            part = pl.ds(pl.multiple_of(128 * t + 64 * half, 64), 64)
            sx1[s, pl.ds(64 * t, 64)] = cp[block, part].astype(jnp.bfloat16)
            x1_copy(t, s).start()

    def add_on(b, e, g):
        t = tile(b, e, g)
        rows = pl.ds(64 * t, 64)
        def act():
            arrived(rx1.at[:, rows], x1r.at[t])
            for s in (0, 1):
                value = cp[block_of(1 if s == 0 else -1), pl.ds(128 * t + 64 * s, 64)]
                sx2[s, rows] = (value + rx1[s, rows].astype(jnp.float32)).astype(jnp.bfloat16)
                x2_copy(t, s).start()
        pl.when(jnp.logical_not(is_target(e)))(act)

    def finish(b, e, g):
        t = tile(b, e, g)
        rows = pl.ds(64 * t, 64)
        def act():
            arrived(rx1.at[:, rows], x1r.at[t])
            arrived(rx2.at[:, rows], x2r.at[t])
            for s in (0, 1):
                total = (
                    cp[block_of(0), pl.ds(128 * t + 64 * s, 64)]
                    + rx2[s, rows].astype(jnp.float32)
                    + rx1[1 - s, rows].astype(jnp.float32)
                ).astype(jnp.bfloat16)
                if g == 0:
                    out[pl.ds(pl.multiple_of(y * 256 + 128 * b + 64 * s, 64), 64)] = total
                else:
                    res[pl.ds(128 * (4 * b + g) + 64 * s, 64)] = total
            if g > 0:
                for h in (0, 1) if g < 3 else (0,):
                    o_copy(b, g, h, dev(dy=owner(g, h))).start()
        pl.when(is_target(e))(act)

    def mask_own():
        for load in loads:
            load.wait()
        row_sym = row_ir[0, 0] ^ row_ir[0, 1]
        for k in (0, 1):
            keep = (row_sym == (col_ir[k, 0] ^ col_ir[k, 1])).astype(jnp.int32).astype(jnp.float32)
            cols = pl.ds(256 * k, 256)
            for s in (0, 1):
                wb[0, s, :, cols] = (wb[0, s, :, cols].astype(jnp.float32) * keep).astype(jnp.bfloat16)

    load_a.wait()
    pl.semaphore_wait(barrier, len(partners))

    def perform(steps):
        for step in steps:
            name, args = step[0], step[1:]
            if name == "zo":
                z_send(args[0], 1)
                give(args[0], 0)
            elif name == "zf":
                z_wait(*args)
                z_send(args[0], args[1] + 1)
                give(*args)
            elif name == "pk":
                pack(*args)
            elif name == "wo":
                for s in (0, 1):
                    y_copy(s, args[0]).start()
            elif name == "wk":
                mask_own()
            elif name == "wg":
                w_give(0).start()
            elif name == "wf":
                arrived(wb.at[args[0] + 1, :, :, pl.ds(0, 512)], yr.at[args[0]])
                if args[0] == 0:
                    for s in (0, 1):
                        y_copy(s, 2).start()
                w_give(args[0] + 1).start()
            elif name == "ws":
                w_give(args[0]).wait_recv()
            elif name == "mm":
                multiply(*args)
            elif name == "ra":
                add_on(*args)
            elif name == "fi":
                finish(*args)

    pl.when(mine)(lambda: perform(STEPS_MINE))
    pl.when(jnp.logical_not(mine))(lambda: perform(STEPS_OTHER))
    arrived(out.at[pl.ds(0, 768)], orr)
    left(ag.at[pl.ds(0, 7)], 0)
    pl.when(mine)(lambda: left(ag.at[pl.ds(0, 4)], 1))
    pl.when(jnp.logical_not(mine))(lambda: left(ag.at[pl.ds(0, 3)], 1))
    left(wb.at[pl.ds(0, 3), :, :, pl.ds(0, 512)], 2)
    left(wb.at[:, :, :, pl.ds(0, 512)], 3)
    left(sx1, 4)
    left(sx2.at[:, pl.ds(0, 512)], 5)
    left(res.at[pl.ds(0, 768)], 6)


STEPS_MINE = [
    ("zo", 0), ("zo", 1), ("wk",), ("wo", 0), ("zo", 2), ("wo", 1), ("zf", 0, 1), ("zf", 1, 1), ("zo", 3), ("wg",),
    ("wf", 0), ("zf", 0, 2), ("zf", 1, 2), ("zf", 2, 1), ("ws", 0), ("ws", 1), ("pk", 0, 0), ("mm", 0, 0, 1),
    ("mm", 0, 0, 0), ("zf", 0, 3), ("zf", 3, 1), ("zf", 1, 3), ("wf", 1), ("ra", 0, 0, 1), ("ra", 0, 0, 0),
    ("zf", 2, 2), ("ws", 2), ("mm", 0, 0, 2), ("zf", 3, 2), ("fi", 0, 0, 1), ("fi", 0, 0, 0), ("pk", 0, 1),
    ("mm", 0, 1, 1), ("mm", 0, 1, 2), ("wf", 2), ("zf", 2, 3), ("ra", 0, 0, 2), ("pk", 1, 0), ("mm", 1, 0, 1),
    ("mm", 1, 0, 2), ("zf", 3, 3), ("ws", 3), ("mm", 0, 0, 3), ("mm", 0, 1, 3), ("mm", 1, 0, 3), ("ra", 0, 1, 1),
    ("ra", 0, 1, 2), ("ra", 1, 0, 1), ("ra", 1, 0, 2), ("pk", 1, 1), ("mm", 1, 1, 3), ("mm", 1, 1, 1),
    ("mm", 1, 1, 2), ("fi", 0, 0, 2), ("fi", 0, 1, 1), ("fi", 0, 1, 2), ("ra", 0, 0, 3), ("ra", 0, 1, 3),
    ("ra", 1, 0, 3), ("mm", 0, 1, 0), ("ra", 1, 1, 3), ("ra", 1, 1, 1), ("ra", 1, 1, 2), ("fi", 1, 0, 1),
    ("fi", 1, 0, 2), ("mm", 1, 0, 0), ("mm", 1, 1, 0), ("fi", 0, 0, 3), ("fi", 0, 1, 3), ("fi", 1, 0, 3),
    ("fi", 1, 1, 3), ("fi", 1, 1, 1), ("fi", 1, 1, 2), ("ra", 0, 1, 0), ("ra", 1, 0, 0), ("ra", 1, 1, 0),
    ("fi", 0, 1, 0), ("fi", 1, 0, 0), ("fi", 1, 1, 0),
]

STEPS_OTHER = [
    ("zo", 0), ("zo", 1), ("wk",), ("wo", 0), ("zo", 2), ("wo", 1), ("zf", 0, 1), ("zf", 1, 1), ("zo", 3), ("wg",),
    ("wf", 0), ("zf", 0, 2), ("zf", 1, 2), ("zf", 2, 1), ("ws", 0), ("ws", 1), ("zf", 0, 3), ("zf", 3, 1),
    ("zf", 1, 3), ("wf", 1), ("zf", 2, 2), ("pk", 0, 0), ("mm", 0, 0, 1), ("mm", 0, 0, 0), ("pk", 0, 1),
    ("mm", 0, 1, 1), ("zf", 3, 2), ("mm", 0, 1, 0), ("ws", 2), ("mm", 0, 0, 2), ("mm", 0, 1, 2), ("ra", 0, 0, 1),
    ("wf", 2), ("zf", 2, 3), ("ra", 0, 0, 0), ("ra", 0, 1, 1), ("ra", 0, 1, 0), ("zf", 3, 3), ("ra", 0, 0, 2),
    ("ra", 0, 1, 2), ("ws", 3), ("mm", 0, 0, 3), ("mm", 0, 1, 3), ("pk", 1, 0), ("pk", 1, 1), ("mm", 1, 0, 3),
    ("mm", 1, 1, 3), ("mm", 1, 0, 1), ("mm", 1, 1, 1), ("mm", 1, 0, 2), ("mm", 1, 1, 2), ("fi", 0, 0, 1),
    ("fi", 0, 1, 1), ("ra", 0, 0, 3), ("ra", 0, 1, 3), ("fi", 0, 0, 2), ("fi", 0, 1, 2), ("ra", 1, 0, 3),
    ("ra", 1, 1, 3), ("fi", 0, 0, 0), ("fi", 0, 1, 0), ("ra", 1, 0, 1), ("ra", 1, 1, 1), ("mm", 1, 0, 0),
    ("mm", 1, 1, 0), ("fi", 0, 0, 3), ("fi", 0, 1, 3), ("ra", 1, 0, 2), ("ra", 1, 1, 2), ("fi", 1, 0, 3),
    ("fi", 1, 1, 3), ("fi", 1, 0, 1), ("fi", 1, 1, 1), ("ra", 1, 0, 0), ("ra", 1, 1, 0), ("fi", 1, 0, 2),
    ("fi", 1, 1, 2), ("fi", 1, 0, 0), ("fi", 1, 1, 0),
]


def on_device(amplitudes, integrals, row_irreps, col_irreps):
    count, bf16, dma = len(CHUNKS), jnp.bfloat16, pltpu.SemaphoreType.DMA
    hbm, vmem = (pl.BlockSpec(memory_space=s) for s in (pltpu.HBM, pltpu.VMEM))
    return pl.pallas_call(
        kernel,
        out_shape=jax.ShapeDtypeStruct((1024, 256), bf16),
        in_specs=[hbm] * 4,
        out_specs=vmem,
        scratch_shapes=[
            pltpu.SMEM((1, 2), jnp.int32),
            pltpu.SMEM((2, 2), jnp.int32),
            pltpu.VMEM((8, 256, 512), bf16),
            pltpu.VMEM((4, 256, 512), bf16),
            pltpu.VMEM((2, 512, 1024), bf16),
            pltpu.VMEM((4, 2, 256, 1024), bf16),
            pltpu.VMEM((2, 2048, 256), jnp.float32),
            pltpu.VMEM((2, 1024, 256), bf16),
            pltpu.VMEM((2, 1024, 256), bf16),
            pltpu.VMEM((2, 1024, 256), bf16),
            pltpu.VMEM((2, 1024, 256), bf16),
            pltpu.VMEM((1024, 256), bf16),
            dma((4,)),
            dma((7,)), dma((count, 3)), dma((count,)), dma((count,)), dma((3,)), dma((4,)), dma((16,)), dma((16,)), dma,
        ],
        compiler_params=pltpu.CompilerParams(
            collective_id=0, has_side_effects=True, vmem_limit_bytes=48 * 2**20
        ),
        cost_estimate=pl.CostEstimate(flops=2 * 2**30, bytes_accessed=2 * 2**20, transcendentals=0),
        name="ladder",
    )(*(pltpu.with_memory_space_constraint(a, pltpu.HBM) for a in (amplitudes, integrals, row_irreps, col_irreps)))


def solution(mesh):
    in_specs = (P("pair", "cd"), P(None, "pair", "cd"), P("pair", None), P("cd", None))
    out_specs = P("cd", "pair")
    return jax.shard_map(
        on_device, mesh=mesh, in_specs=in_specs, out_specs=out_specs, check_vma=False
    )
```
